32 devices in a mesh: grp: 2 (over core), dom: 16 (over z, y, x).
Axes of the slice: x: 2, y: 2, z: 4, core: 2. Of those that a mesh axis runs over, the one named last changes fastest.
Arguments:
- flow_temp: float32 [128, 512, 256], P(None, ('grp', 'dom')), may hold values from -6 to 6
- velocity: bfloat16 [3, 128, 512, 256], P(None, None, ('grp', 'dom')), may hold values from -2.5 to 2.5
- heat_release: bfloat16 [128, 512, 256], P(None, ('grp', 'dom')), may hold values from 0.049804688 to 2
- solid_temp: float32 [32, 512, 256], P(None, ('grp', 'dom')), may hold values from -6 to 6
- conductivity: float32 [32, 512, 256], P(None, ('grp', 'dom')), may hold values from 0.5 to 2
- interp_table: float32 [16, 16, 1024], replicated, may hold values from -0.375 to 0.375
- flow_patch: int32 [131072], P(('grp', 'dom')), may hold values from 0 to 255
- solid_device: int32 [131072, 1], P(('grp', 'dom')), may hold values from 0 to 31; in each aligned block of 4096 rows (0 to 4095, 4096 to 8191, ...) at most 256 rows name the same one
- solid_patch: int32 [131072], P(('grp', 'dom')), may hold values from 0 to 255
- block_index: int32 [131072], P(('grp', 'dom')), may hold values from 0 to 1023
Outputs:
- flow_out: float32 [128, 512, 256], P(None, ('grp', 'dom'))
- solid_out: float32 [32, 512, 256], P(None, ('grp', 'dom'))
The draws below stay inside these ranges and needn't reach their ends.
Inputs may be any that keep to these rules, and one draw needn't show every extreme that they name: `solid_device`: within the 4096 rows of one device no liner device is named more than 256 times, and some liner device is named exactly 256 times.
All inputs are finite; a program needn't handle non-finite values.
Results may differ from the reference program's by a relative error of at most 0.00115.
Values may be sent and summed in bfloat16 or wider, within the bound.
No kernel may reach another device: no remote copies, remote signals or barrier semaphores. Data moves between devices by JAX's collectives and lax.ppermute only.
A program may use at most 128 MiB of HBM per device.

```python
import math
import jax
import jax.numpy as jnp
import numpy as np
from jax import lax

NY = 256
NZF = 128
NZS = 32
SUBCYCLES = 4
NB = 1024
PF = 256
OV_DEV = 4096
CAP = 256
NXF = 512
PATCHES = 8192
CORRELATIONS = 131072
N_GRP = 2
N_DOM = 16
DEVICES = 32


def place_ends(array, stream_key, low, largest):
    dims = array.shape
    place = [jax.random.randint(jax.random.fold_in(stream_key, axis), (), 0, dims[axis]) for axis in range(len(dims))]
    array = array.at[tuple(place)].set(low)
    longest = dims.index(max(dims))
    place[longest] = (place[longest] + 1) % dims[longest]
    return array.at[tuple(place)].set(largest)


def shard_levels(rng, dims, cuts, smallest, top_value):
    factor_of = 1.0
    for position, blocks in cuts:
        draws = jax.random.uniform(jax.random.fold_in(jax.random.fold_in(rng, 6), position), (blocks,), jnp.float32, smallest / len(cuts), top_value / len(cuts))
        factor_of = factor_of * jnp.repeat(jnp.exp(draws), dims[position] // blocks).reshape((-1,) + (1,) * (len(dims) - 1 - position))
    return factor_of


def deal_out(own_key, own, number, rows, amount, top, reach, lean):
    ranking = jax.random.permutation(own_key, amount)
    heavy_load, ordinary = load_shares(amount, rows * top, reach, lean, True), load_shares(amount, rows * top, reach, lean, False)
    places = jnp.arange(amount)

    def named(lengths, rotation):
        used = int((lengths > 0).sum())
        fixed = max(1, used // 4)
        passed = fixed + (places - fixed + rotation * (used - fixed)) % max(1, amount - fixed)
        return jnp.zeros((amount,), jnp.int32).at[ranking[jnp.where(places < fixed, places, passed)]].set(jnp.asarray(lengths, jnp.int32))

    lengths = jnp.where(number % 4 == 0, named(heavy_load, number // 4), named(ordinary, number - number // 4 - 1))
    mixed = jax.random.permutation(jax.random.fold_in(own, 3), amount)
    giver, sink = mixed[0:amount // 2 * 2:2], mixed[1:amount // 2 * 2:2]
    slack = jnp.minimum(lengths[giver] - 1, reach - lengths[sink]) // 2
    slack = jnp.where((giver == ranking[0]) | (sink == ranking[0]) | (lengths[sink] == 0), 0, jnp.maximum(slack, 0))
    passed = jax.random.randint(jax.random.fold_in(own, 4), (amount // 2,), 0, 1 << 20) % (slack + 1)
    lengths = lengths.at[giver].add(-passed).at[sink].add(passed)
    members = jnp.searchsorted(jnp.cumsum(lengths), jnp.arange(rows * top), side="right").astype(jnp.int32)
    table = members.reshape(top, rows).T
    table = table[jax.random.permutation(jax.random.fold_in(own, 1), rows)]
    rotation = jax.random.randint(jax.random.fold_in(own, 2), (rows, 1), 0, top)
    return jnp.take_along_axis(table, (jnp.arange(top)[None, :] + rotation) % top, axis=1)


def load_shares(amount, total, limit, lean, full):
    portions = [(1 << 20) // math.isqrt(rank ** lean) + 1 for rank in range(1, amount + 1)]
    largest = limit if full else min(limit, max(-(-total // amount), total * portions[0] // sum(portions)))
    least = 1 if total - largest >= amount - 1 else 0
    holding, surplus = [largest] + [least] * (amount - 1), total - largest - least * (amount - 1)
    while surplus > 0:
        free = [i for i in range(1, amount) if holding[i] < largest] or [i for i in range(1, amount) if holding[i] < limit]
        whole, budget = sum([portions[i] for i in free]), surplus
        for i in free:
            more = min(limit - holding[i], max(1, budget * portions[i] // whole), surplus)
            holding[i] = holding[i] + more
            surplus = surplus - more
    return np.array(holding)


def noise(rng, shape, deviation, limit, cuts=(), kind=jnp.bfloat16):
    result = jax.random.normal(rng, shape, jnp.float32) * deviation
    if len(cuts) > 0:
        result = shard_levels(rng, shape, cuts, -0.22, 0.18) * result
    return jnp.clip(result, min=-limit, max=limit).astype(kind)


def setup_inputs(seed: int = 0) -> dict:
    key_of = jax.random.split(jax.random.key(seed), 11)
    flow_temp = noise(key_of[0], (NZF, NXF, NY), 1.0, 6.0, ((1, 32),), jnp.float32)
    velocity = noise(key_of[1], (3, NZF, NXF, NY), 0.7, 2.5, ((2, 32),))
    heat_release = jnp.clip(jnp.exp(math.log(2.0) - 3.6927934 * jax.random.uniform(key_of[2], (NZF, NXF, NY), jnp.float32) ** shard_levels(key_of[2], (NZF, NXF, NY), ((1, 32),), -0.2, 0.2)), 0.049804688, 2.0).astype(jnp.bfloat16)
    solid_temp = noise(key_of[3], (NZS, NXF, NY), 1.0, 6.0, ((1, 32),), jnp.float32)
    conductivity = jnp.clip(jnp.exp(math.log(2.0) - 1.3862944 * jax.random.uniform(key_of[4], (NZS, NXF, NY), jnp.float32) ** shard_levels(key_of[4], (NZS, NXF, NY), ((1, 32),), -0.2, 0.2)), 0.5, 2.0)
    interp_table = noise(key_of[5], (16, 16, NB), 256 ** -0.5, 0.375, (), jnp.float32)
    flow_patch = place_ends(jax.random.randint(key_of[6], (CORRELATIONS,), 0, PF), jax.random.fold_in(key_of[6], 1), 0, PF - 1).astype(jnp.int32)
    solid_device_keys = jax.random.split(jax.random.fold_in(key_of[7], 1), CORRELATIONS // OV_DEV)
    solid_device_turns = jax.random.permutation(jax.random.fold_in(key_of[7], 3), CORRELATIONS // OV_DEV)
    solid_device = jax.vmap(lambda own, number: deal_out(jax.random.fold_in(key_of[7], 2), own, number, OV_DEV, DEVICES, 1, CAP, 2))(solid_device_keys, solid_device_turns).reshape((CORRELATIONS, 1))
    solid_patch = place_ends(jax.random.randint(key_of[8], (CORRELATIONS,), 0, PF), jax.random.fold_in(key_of[8], 1), 0, PF - 1).astype(jnp.int32)
    block_index = place_ends(jax.random.randint(key_of[9], (CORRELATIONS,), 0, NB), jax.random.fold_in(key_of[9], 1), 0, NB - 1).astype(jnp.int32)
    return {"flow_temp": flow_temp, "velocity": velocity, "heat_release": heat_release, "solid_temp": solid_temp, "conductivity": conductivity, "interp_table": interp_table, "flow_patch": flow_patch, "solid_device": solid_device, "solid_patch": solid_patch, "block_index": block_index}


DIFFUSION = 0.8
TIMESTEP = 0.12
FILM_COEFF = 1.0
CONDUCT_RATE = 0.08
FLUX_GAIN = 0.25
slab_depth = 8


def to_patches(face_values):
    rows_x, cols_y = face_values.shape
    return face_values.reshape(rows_x, cols_y // 16, 16).transpose(2, 0, 1).reshape(16, rows_x * (cols_y // 16))


def from_patches(patches, rows_x):
    per_row = patches.shape[1] // rows_x
    return patches.reshape(16, rows_x, per_row).transpose(1, 2, 0).reshape(rows_x, per_row * 16)


def upwind(component, centre, lower_side, upper_side):
    return jnp.maximum(component, 0.0) * (centre - lower_side) + jnp.minimum(component, 0.0) * (upper_side - centre)


def tendency(centre, zbelow, zabove, xbelow, xabove, velocity, source):
    ybelow = jnp.roll(centre, 1, axis=2)
    yabove = jnp.roll(centre, -1, axis=2)
    advect = upwind(velocity[0], centre, zbelow, zabove) + upwind(velocity[1], centre, xbelow, xabove)
    advect = advect + upwind(velocity[2], centre, ybelow, yabove)
    spread = zbelow + zabove + xbelow + xabove + ybelow + yabove - 6.0 * centre
    return source - advect + DIFFUSION * spread


def flow_tendency(current, wall_face, velocity, heat_release):
    padded = jnp.concatenate([jnp.zeros_like(current[:1]), current, wall_face[None]], 0)

    def compute_slab(offset):
        slab_rows = lax.dynamic_slice_in_dim(padded, offset, slab_depth + 2, 0)
        centre = slab_rows[1:-1]
        speeds = lax.dynamic_slice_in_dim(velocity, offset, slab_depth, 1).astype(jnp.float32)
        source = lax.dynamic_slice_in_dim(heat_release, offset, slab_depth, 0).astype(jnp.float32)
        return tendency(centre, slab_rows[:-2], slab_rows[2:], jnp.roll(centre, 1, axis=1), jnp.roll(centre, -1, axis=1), speeds, source)

    offsets = jnp.arange(NZF // slab_depth, dtype=jnp.int32) * slab_depth
    return lax.map(compute_slab, offsets).reshape(current.shape)


def solid_update(current, xbelow, xabove, conduct, flux_face):
    zbelow = jnp.concatenate([current[:1], current[:-1]], 0)
    zabove = jnp.concatenate([current[1:], jnp.zeros_like(current[:1])], 0)
    ybelow = jnp.roll(current, 1, axis=2)
    yabove = jnp.roll(current, -1, axis=2)
    spread = zbelow + zabove + xbelow + xabove + ybelow + yabove - 6.0 * current
    updated = current + CONDUCT_RATE * conduct * spread
    return updated + jnp.concatenate([(FLUX_GAIN * flux_face)[None], jnp.zeros_like(current[1:])], 0)


def reference(flow_temp, velocity, heat_release, solid_temp, conductivity, interp_table, flow_patch, solid_device, solid_patch, block_index):
    devices = N_GRP * N_DOM
    owners = jnp.arange(CORRELATIONS, dtype=jnp.int32) // OV_DEV
    flow_index = (owners * PF + flow_patch).astype(jnp.int32)
    solid_index = (solid_device[:, 0] * PF + solid_patch).astype(jnp.int32)
    solid_wall = to_patches(solid_temp[0])

    def forward_block(pieces):
        blocks, places = pieces
        weights = jnp.take(interp_table, blocks, axis=2)
        return jnp.sum(weights * jnp.take(solid_wall, places, axis=1)[None, :, :], axis=1)

    forward = lax.map(forward_block, (block_index.reshape(devices, OV_DEV), solid_index.reshape(devices, OV_DEV)))
    forward = jnp.transpose(forward, (1, 0, 2)).reshape(16, CORRELATIONS)
    wall_temp = jnp.zeros((16, PATCHES), jnp.float32).at[:, flow_index].add(forward)
    wall_face = from_patches(wall_temp, NXF)
    predictor = flow_temp + TIMESTEP * flow_tendency(flow_temp, wall_face, velocity, heat_release)
    flow_out = 0.5 * flow_temp + 0.5 * (predictor + TIMESTEP * flow_tendency(predictor, wall_face, velocity, heat_release))
    wall_flux = to_patches(FILM_COEFF * (flow_out[-1] - wall_face))

    def backward_block(pieces):
        blocks, places = pieces
        weights = jnp.take(interp_table, blocks, axis=2)
        return jnp.sum(weights * jnp.take(wall_flux, places, axis=1)[:, None, :], axis=0)

    backward = lax.map(backward_block, (block_index.reshape(devices, OV_DEV), flow_index.reshape(devices, OV_DEV)))
    backward = jnp.transpose(backward, (1, 0, 2)).reshape(16, CORRELATIONS)
    solid_flux = jnp.zeros((16, PATCHES), jnp.float32).at[:, solid_index].add(backward)
    flux_face = from_patches(solid_flux, NXF)
    current = solid_temp
    for substep in range(SUBCYCLES):
        current = solid_update(current, jnp.roll(current, 1, axis=1), jnp.roll(current, -1, axis=1), conductivity, flux_face)
    return flow_out, current
```

```python
import functools

import jax
import jax.numpy as jnp
from jax import lax
from jax.experimental import pallas as pl
from jax.experimental.pallas import tpu as pltpu
from jax.sharding import PartitionSpec as P

SUBCYCLES = 4
DIFFUSION = 0.8
TIMESTEP = 0.12
FILM_COEFF = 1.0
CONDUCT_RATE = 0.08
FLUX_GAIN = 0.25

AXES = ("grp", "dom")
NODES = 16
CHUNK = 512
LANES = 128
LAYERS = 16
HALO = 4
F32 = jnp.float32
BF16 = jnp.bfloat16
VMEM_LIMIT = 58 * 1024 * 1024
STEPS_PER_UNIT = 5461.0
I16 = jnp.int16


def params(**kw):
    return pltpu.CompilerParams(vmem_limit_bytes=VMEM_LIMIT, **kw)


def cost(flops, nbytes):
    return pl.CostEstimate(flops=flops, bytes_accessed=nbytes, transcendentals=0)


def one_hot(index, rows):
    cells = lax.broadcasted_iota(jnp.int32, (rows, index.shape[1]), 0)
    return jnp.where(cells == index, 1.0, 0.0).astype(BF16)


def dot(a, b):
    return lax.dot_general(a, b, (((1,), (0,)), ((), ())), preferred_element_type=F32)


def dot_nt(a, b):
    return lax.dot_general(a, b, (((1,), (1,)), ((), ())), preferred_element_type=F32)


def split(x):
    high = x.astype(BF16)
    return high, (x - high.astype(F32)).astype(BF16)


def weights_kernel(block_ref, table_ref, out_ref, table_high, table_low):
    @pl.when(pl.program_id(0) == 0)
    def _():
        table_high[...], table_low[...] = split(table_ref[...])

    picked = one_hot(block_ref[...], table_ref.shape[1])
    out_ref[...] = dot(table_high[...], picked) + dot(table_low[...], picked)


def weights_of(block_index, table):
    entries, blocks = table.shape
    count = block_index.shape[1]
    return pl.pallas_call(
        weights_kernel,
        grid=(count // CHUNK,),
        in_specs=[
            pl.BlockSpec((1, CHUNK), lambda i: (0, i)),
            pl.BlockSpec((entries, blocks), lambda i: (0, 0)),
        ],
        out_specs=pl.BlockSpec((entries, CHUNK), lambda i: (0, i)),
        out_shape=jax.ShapeDtypeStruct((entries, count), F32),
        scratch_shapes=[pltpu.VMEM((entries, blocks), BF16)] * 2,
        compiler_params=params(),
        cost_estimate=cost(4 * entries * blocks * count, 4 * entries * (blocks + count)),
        name="weights",
    )(block_index, table)


def spread_rows(rows_x):
    p = lax.broadcasted_iota(jnp.int32, (rows_x, rows_x * NODES), 1)
    x = lax.broadcasted_iota(jnp.int32, (rows_x, rows_x * NODES), 0)
    return jnp.where(p // NODES == x, 1.0, 0.0).astype(BF16)


def patches_to_face(patches, rows_x):
    count = patches.shape[1]
    c = lax.broadcasted_iota(jnp.int32, (NODES, count), 1) % NODES
    parts = [jnp.where(c == k, patches, 0.0) for k in range(NODES)]
    high, low = split(jnp.concatenate(parts, axis=0))
    rows = spread_rows(rows_x)
    return dot_nt(rows, high) + dot_nt(rows, low)


def face_to_patches(face, rows_x):
    high, low = split(face)
    rows = spread_rows(rows_x)
    wide = lax.dot_general(
        high, rows, (((0,), (0,)), ((), ())), preferred_element_type=F32
    ) + lax.dot_general(low, rows, (((0,), (0,)), ((), ())), preferred_element_type=F32)
    c = lax.broadcasted_iota(jnp.int32, (NODES, rows.shape[1]), 1) % NODES
    out = jnp.zeros((NODES, rows.shape[1]), F32)
    for k in range(NODES):
        out = jnp.where(c == k, wide[k * NODES : (k + 1) * NODES], out)
    return out


def solid_place(device_ref, patch_ref, rows_x):
    per_row = NODES
    patch = patch_ref[...]
    return device_ref[...] * rows_x + patch // per_row, patch % per_row


def forward_kernel(
    device_ref,
    patch_ref,
    flow_p_ref,
    weights_ref,
    faces_ref,
    wall_ref,
    first_ref,
    last_ref,
    faces_high,
    faces_low,
    fetched,
    product_high,
    product_low,
    total,
):
    step = pl.program_id(0)
    rows_x = wall_ref.shape[0]

    @pl.when(step == 0)
    def _():
        faces_high[...], faces_low[...] = split(faces_ref[...].astype(F32).T)
        total[...] = jnp.zeros_like(total)

    solid_x, solid_c = solid_place(device_ref, patch_ref, rows_x)
    picked = one_hot(solid_x, faces_ref.shape[0])
    fetched[...] = dot(faces_high[...], picked) + dot(faces_low[...], picked)
    for k in range(CHUNK // LANES):
        lanes = slice(k * LANES, (k + 1) * LANES)
        c = jnp.broadcast_to(solid_c[:, lanes], (NODES, LANES))
        values = jnp.zeros((NODES, LANES), F32)
        for j in range(NODES):
            values = jnp.where(c == j, fetched[j * NODES : (j + 1) * NODES, lanes], values)
        values = values * (1.0 / STEPS_PER_UNIT)
        for i in range(NODES):
            rows = slice(i * NODES, (i + 1) * NODES)
            product_high[rows, lanes], product_low[rows, lanes] = split(weights_ref[rows, lanes] * values)
    placed = one_hot(flow_p_ref[...], total.shape[1])
    total[...] += dot_nt(product_high[...], placed) + dot_nt(product_low[...], placed)

    @pl.when(step == pl.num_programs(0) - 1)
    def _():
        patches = jnp.sum(total[...].reshape(NODES, NODES, total.shape[1]), axis=1)
        wall = patches_to_face(patches, rows_x)
        wall_ref[...] = wall
        first_ref[...] = wall[:1]
        last_ref[...] = wall[rows_x - 1 :]


def forward(solid_device, solid_patch, flow_p, weights, faces, rows_x):
    entries, count = weights.shape
    tall, width = faces.shape
    line = pl.BlockSpec((1, CHUNK), lambda i: (0, i))
    fixed = lambda shape: pl.BlockSpec(shape, lambda i: (0,) * len(shape))
    return pl.pallas_call(
        forward_kernel,
        grid=(count // CHUNK,),
        in_specs=[
            line,
            line,
            line,
            pl.BlockSpec((entries, CHUNK), lambda i: (0, i)),
            fixed((tall, width)),
        ],
        out_specs=[fixed((rows_x, width)), fixed((1, width)), fixed((1, width))],
        out_shape=[
            jax.ShapeDtypeStruct((rows_x, width), F32),
            jax.ShapeDtypeStruct((1, width), F32),
            jax.ShapeDtypeStruct((1, width), F32),
        ],
        scratch_shapes=[
            pltpu.VMEM((width, tall), BF16),
            pltpu.VMEM((width, tall), BF16),
            pltpu.VMEM((width, CHUNK), F32),
            pltpu.VMEM((entries, CHUNK), BF16),
            pltpu.VMEM((entries, CHUNK), BF16),
            pltpu.VMEM((entries, rows_x * NODES), F32),
        ],
        compiler_params=params(),
        cost_estimate=cost(4 * width * (tall + entries) * count, 4 * entries * count),
        name="forward",
    )(solid_device, solid_patch, flow_p, weights, faces)


def edges_kernel(
    flow_low_ref, flow_high_ref, speed_ref, solid_ref, rates_ref, up_ref, down_ref
):
    layers = flow_low_ref.shape[0]
    solid_layers, rows, width = solid_ref.shape
    low = lax.broadcasted_iota(jnp.int32, (8, width), 0) < HALO
    for l in range(0, solid_layers, 2):
        ups, downs = [], []
        for m in (l, l + 1):
            ups.append(
                jnp.where(low, pltpu.roll(rates_ref[m, rows - 8 :], HALO, 0), solid_ref[m, rows - 8 :])
            )
            downs.append(jnp.where(low, solid_ref[m, :8], pltpu.roll(rates_ref[m, :8], HALO, 0)))
        up_ref[l * 8 : l * 8 + 16] = jnp.concatenate(ups, axis=0).astype(BF16)
        down_ref[l * 8 : l * 8 + 16] = jnp.concatenate(downs, axis=0).astype(BF16)
    start = solid_layers * 8
    for l in range(0, layers, LAYERS):
        part = slice(start + l, start + l + LAYERS)
        up_ref[part] = jnp.concatenate(
            [flow_high_ref[m, 7:8] for m in range(l, l + LAYERS)], axis=0
        ).astype(BF16)
        down_ref[part] = jnp.concatenate(
            [flow_low_ref[m, 0:1] for m in range(l, l + LAYERS)], axis=0
        ).astype(BF16)
    part = slice(start + layers, start + layers + LAYERS)
    speed = speed_ref[0, 0].astype(F32)
    up_ref[part] = jnp.broadcast_to(speed[rows - 1 :], (LAYERS, width)).astype(BF16)
    down_ref[part] = jnp.broadcast_to(speed[:1], (LAYERS, width)).astype(BF16)


def edges(flow, velocity, solid, rates):
    layers, rows, width = flow.shape
    solid_layers = solid.shape[0]
    shape = (solid_layers * 8 + layers + LAYERS, width)
    whole = pl.BlockSpec(solid.shape, lambda i: (0, 0, 0))
    return pl.pallas_call(
        edges_kernel,
        grid=(1,),
        in_specs=[
            pl.BlockSpec((layers, 8, width), lambda i: (0, 0, 0)),
            pl.BlockSpec((layers, 8, width), lambda i: (0, rows // 8 - 1, 0)),
            pl.BlockSpec((1, 1, rows, width), lambda i: (0, layers - 1, 0, 0)),
            whole,
            whole,
        ],
        out_specs=[pl.BlockSpec(shape, lambda i: (0, 0))] * 2,
        out_shape=[jax.ShapeDtypeStruct(shape, BF16)] * 2,
        compiler_params=params(),
        cost_estimate=cost(8 * shape[0] * width, 12 * shape[0] * width),
        name="edges",
    )(flow, flow, velocity, solid, rates)


def layer_tendency(centre, zlow, zhigh, xlow, xhigh, vz, vx, vy, source):
    width = centre.shape[1]
    total = source
    pairs = (
        (vz, zlow, zhigh),
        (vx, xlow, xhigh),
        (vy, pltpu.roll(centre, 1, 1), pltpu.roll(centre, width - 1, 1)),
    )
    for speed, low, high in pairs:
        a = jnp.maximum(speed, 0.0) + DIFFUSION
        b = a - speed
        total = total + a * (low - centre) + b * (high - centre)
    return total


def x_neighbours(centre, low_row, high_row):
    rows, width = centre.shape
    row = lax.broadcasted_iota(jnp.int32, (rows, width), 0)
    low = jnp.where(row == 0, jnp.broadcast_to(low_row, (rows, width)), pltpu.roll(centre, 1, 0))
    high = jnp.where(
        row == rows - 1, jnp.broadcast_to(high_row, (rows, width)), pltpu.roll(centre, rows - 1, 0)
    )
    return low, high


def predictor_kernel(
    below_ref, flow_ref, above_ref, low_ref, high_ref, velocity_ref, heat_ref, out_ref, first_ref, last_ref
):
    step = pl.program_id(0)
    lows = low_ref[...].astype(F32)
    highs = high_ref[...].astype(F32)
    first, last = [], []
    rows = flow_ref.shape[1]
    for l in range(LAYERS):
        centre = flow_ref[l]
        if l == 0:
            zlow = jnp.where(step == 0, 0.0, below_ref[0])
        else:
            zlow = flow_ref[l - 1]
        if l == LAYERS - 1:
            zhigh = jnp.where(step == pl.num_programs(0) - 1, 0.0, above_ref[0])
        else:
            zhigh = flow_ref[l + 1]
        xlow, xhigh = x_neighbours(centre, lows[l : l + 1], highs[l : l + 1])
        vz, vx, vy = (velocity_ref[d, l].astype(F32) for d in range(3))
        value = centre + TIMESTEP * layer_tendency(
            centre, zlow, zhigh, xlow, xhigh, vz, vx, vy, heat_ref[l].astype(F32)
        )
        out_ref[l] = value
        first.append(value[0:1])
        last.append(value[rows - 1 : rows])
    first_ref[...] = jnp.concatenate(first, axis=0).astype(BF16)
    last_ref[...] = jnp.concatenate(last, axis=0).astype(BF16)


def layer_specs(shape, halo=True):
    layers, rows, width = shape
    block = pl.BlockSpec((LAYERS, rows, width), lambda i: (i, 0, 0))
    below = pl.BlockSpec((1, rows, width), lambda i: (jnp.maximum(i * LAYERS - 1, 0), 0, 0))
    above = pl.BlockSpec((1, rows, width), lambda i: (jnp.minimum((i + 1) * LAYERS, layers - 1), 0, 0))
    speeds = pl.BlockSpec((3, LAYERS, rows, width), lambda i: (0, i, 0, 0))
    edge = pl.BlockSpec((LAYERS, width), lambda i: (i, 0))
    return block, below, above, speeds, edge


def predictor(flow, low, high, velocity, heat):
    layers, rows, width = flow.shape
    block, below, above, speeds, edge = layer_specs(flow.shape)
    cells = layers * rows * width
    first_edge = low.shape[0] // LAYERS - layers // LAYERS - 1
    flow_edge = pl.BlockSpec((LAYERS, width), lambda i: (i + first_edge, 0))
    return pl.pallas_call(
        predictor_kernel,
        grid=(layers // LAYERS,),
        in_specs=[below, block, above, flow_edge, flow_edge, speeds, block],
        out_specs=[block, edge, edge],
        out_shape=[
            jax.ShapeDtypeStruct(flow.shape, F32),
            jax.ShapeDtypeStruct((layers, width), BF16),
            jax.ShapeDtypeStruct((layers, width), BF16),
        ],
        compiler_params=params(),
        cost_estimate=cost(40 * cells, 16 * cells),
        name="predictor",
    )(flow, flow, flow, low, high, velocity, heat)


def corrector_kernel(
    below_ref, mid_ref, above_ref, top_ref, wall_ref, rim_ref, low_ref, high_ref, flow_ref, velocity_ref, heat_ref, out_ref
):
    step = pl.program_id(0)
    final = step == pl.num_programs(0) - 1
    lows = low_ref[...].astype(F32)
    highs = high_ref[...].astype(F32)
    for l in range(LAYERS):
        centre = mid_ref[l]
        low_row, high_row = lows[l : l + 1], highs[l : l + 1]
        zlow = jnp.where(step == 0, 0.0, below_ref[0]) if l == 0 else mid_ref[l - 1]
        if l == LAYERS - 1:
            centre = jnp.where(final, top_ref[...], centre)
            zhigh = jnp.where(final, wall_ref[...], above_ref[0])
            low_row = jnp.where(final, rim_ref[0:1], low_row)
            high_row = jnp.where(final, rim_ref[1:2], high_row)
        elif l == LAYERS - 2:
            zhigh = jnp.where(final, top_ref[...], mid_ref[l + 1])
        else:
            zhigh = mid_ref[l + 1]
        xlow, xhigh = x_neighbours(centre, low_row, high_row)
        vz, vx, vy = (velocity_ref[d, l].astype(F32) for d in range(3))
        slope = layer_tendency(centre, zlow, zhigh, xlow, xhigh, vz, vx, vy, heat_ref[l].astype(F32))
        out_ref[l] = 0.5 * flow_ref[l] + 0.5 * (centre + TIMESTEP * slope)


def corrector(mid, top, wall, rim, low, high, flow, velocity, heat):
    layers, rows, width = flow.shape
    block, below, above, speeds, edge = layer_specs(flow.shape)
    face = pl.BlockSpec((rows, width), lambda i: (0, 0))
    cells = layers * rows * width
    return pl.pallas_call(
        corrector_kernel,
        grid=(layers // LAYERS,),
        in_specs=[below, block, above, face, face, pl.BlockSpec(rim.shape, lambda i: (0, 0)), edge, edge, block, speeds, block],
        out_specs=block,
        out_shape=jax.ShapeDtypeStruct(flow.shape, F32),
        compiler_params=params(),
        cost_estimate=cost(44 * cells, 20 * cells),
        name="corrector",
    )(mid, mid, mid, top, wall, rim, low, high, flow, velocity, heat)


def backward_kernel(
    device_ref,
    patch_ref,
    flow_p_ref,
    weights_ref,
    wall_ref,
    wall_low_ref,
    wall_high_ref,
    vz_low_ref,
    vz_high_ref,
    mid_ref,
    low_ref,
    high_ref,
    flow_ref,
    velocity_ref,
    heat_ref,
    send_ref,
    top_ref,
    rim_ref,
    flux_high,
    flux_low,
    fetched,
    returned_high,
    returned_low,
    total,
):
    step = pl.program_id(0)
    rows, width = wall_ref.shape

    @pl.when(step == 0)
    def _():
        total[...] = jnp.zeros_like(total)
        wall = wall_ref[...]
        vz, vx, vy = (velocity_ref[d, 0].astype(F32) for d in range(3))
        top = mid_ref[1] + TIMESTEP * (DIFFUSION - jnp.minimum(vz, 0.0)) * wall
        edge = low_ref.shape[0]
        low_row = low_ref[edge - 1 : edge].astype(F32) + TIMESTEP * (
            DIFFUSION - jnp.minimum(vz_low_ref[...].astype(F32)[:1], 0.0)
        ) * wall_low_ref[...]
        high_row = high_ref[edge - 1 : edge].astype(F32) + TIMESTEP * (
            DIFFUSION - jnp.minimum(vz_high_ref[...].astype(F32)[:1], 0.0)
        ) * wall_high_ref[...]
        xlow, xhigh = x_neighbours(top, low_row, high_row)
        slope = layer_tendency(top, mid_ref[0], wall, xlow, xhigh, vz, vx, vy, heat_ref[0].astype(F32))
        out = 0.5 * flow_ref[0] + 0.5 * (top + TIMESTEP * slope)
        top_ref[...] = top
        rim_ref[...] = jnp.zeros_like(rim_ref)
        rim_ref[0:1] = low_row
        rim_ref[1:2] = high_row
        patches = face_to_patches(FILM_COEFF * (out - wall), rows)
        wide = jnp.broadcast_to(patches[:, None, :], (NODES, NODES, patches.shape[1]))
        high, low = split(wide.reshape(NODES * NODES, patches.shape[1]))
        flux_high[...] = high
        flux_low[...] = low

    picked = one_hot(flow_p_ref[...], flux_high.shape[1])
    fetched[...] = dot(flux_high[...], picked) + dot(flux_low[...], picked)
    solid_x, solid_c = solid_place(device_ref, patch_ref, rows)
    for k in range(CHUNK // LANES):
        lanes = slice(k * LANES, (k + 1) * LANES)
        value = jnp.zeros((NODES, LANES), F32)
        for i in range(NODES):
            part = slice(i * NODES, (i + 1) * NODES)
            value = value + weights_ref[part, lanes] * fetched[part, lanes]
        c = jnp.broadcast_to(solid_c[:, lanes], (NODES, LANES))
        high, low = split(value)
        high, low = high.astype(F32), low.astype(F32)
        for j in range(NODES):
            part = slice(j * NODES, (j + 1) * NODES)
            returned_high[part, lanes] = jnp.where(c == j, high, 0.0).astype(BF16)
            returned_low[part, lanes] = jnp.where(c == j, low, 0.0).astype(BF16)
    placed = one_hot(solid_x, total.shape[0])
    total[...] += dot_nt(placed, returned_high[...]) + dot_nt(placed, returned_low[...])

    @pl.when(step == pl.num_programs(0) - 1)
    def _():
        devices = send_ref.shape[0]
        tall = total.shape[0]
        peak = jnp.zeros((8, width), F32)
        for r in range(0, tall, 8):
            peak = jnp.maximum(peak, jnp.abs(total[r : r + 8]))
        peak = jnp.maximum(jnp.max(peak, axis=0, keepdims=True), 1e-30)
        power = jnp.floor(jnp.log2(peak)) + 1.0
        factor = jnp.exp2(15.0 - power)
        sub = lax.broadcasted_iota(jnp.int32, (8, width), 0)
        for d in range(devices):
            own = total[d * rows : (d + 1) * rows]
            after = ((d + 1) * rows) % tall
            before = (d * rows - 8) % tall
            rim = jnp.where(sub < HALO, total[after : after + 8], total[before : before + 8])
            scaled = jnp.clip(jnp.round(jnp.concatenate([own, rim], axis=0) * factor), -32767.0, 32767.0)
            place = lax.broadcasted_iota(jnp.int32, scaled.shape, 0) == rows + HALO - 1
            scaled = jnp.where(place, jnp.broadcast_to(power, scaled.shape), scaled)
            send_ref[d] = scaled.astype(jnp.int32).astype(I16)


def backward(solid_device, solid_patch, flow_p, weights, wall, wall_low, wall_high, edge_low, edge_high, mid, low, high, flow, velocity, heat, devices):
    entries, count = weights.shape
    rows, width = wall.shape
    layers = flow.shape[0]
    tall = devices * rows
    line = pl.BlockSpec((1, CHUNK), lambda i: (0, i))
    fixed = lambda shape: pl.BlockSpec(shape, lambda i: (0,) * len(shape))
    edge = pl.BlockSpec((LAYERS, width), lambda i: (layers // LAYERS - 1, 0))
    last = edge_low.shape[0] // LAYERS - 1
    speed = pl.BlockSpec((LAYERS, width), lambda i: (last, 0))
    return pl.pallas_call(
        backward_kernel,
        grid=(count // CHUNK,),
        in_specs=[
            line,
            line,
            line,
            pl.BlockSpec((entries, CHUNK), lambda i: (0, i)),
            fixed((rows, width)),
            fixed((1, width)),
            fixed((1, width)),
            speed,
            speed,
            pl.BlockSpec((2, rows, width), lambda i: (layers // 2 - 1, 0, 0)),
            edge,
            edge,
            pl.BlockSpec((1, rows, width), lambda i: (layers - 1, 0, 0)),
            pl.BlockSpec((3, 1, rows, width), lambda i: (0, layers - 1, 0, 0)),
            pl.BlockSpec((1, rows, width), lambda i: (layers - 1, 0, 0)),
        ],
        out_specs=[fixed((devices, rows + 8, width)), fixed((rows, width)), fixed((8, width))],
        out_shape=[
            jax.ShapeDtypeStruct((devices, rows + 8, width), I16),
            jax.ShapeDtypeStruct((rows, width), F32),
            jax.ShapeDtypeStruct((8, width), F32),
        ],
        scratch_shapes=[
            pltpu.VMEM((entries, rows * NODES), BF16),
            pltpu.VMEM((entries, rows * NODES), BF16),
            pltpu.VMEM((entries, CHUNK), F32),
            pltpu.VMEM((width, CHUNK), BF16),
            pltpu.VMEM((width, CHUNK), BF16),
            pltpu.VMEM((tall, width), F32),
        ],
        compiler_params=params(),
        cost_estimate=cost(4 * width * (tall + entries) * count, 4 * entries * count),
        name="backward",
    )(solid_device, solid_patch, flow_p, weights, wall, wall_low, wall_high, edge_low, edge_high, mid, low, high, flow, velocity, heat)


def conduct(current, layers, rates, flux):
    rows = current[0].shape[0]
    width = current[0].shape[1]
    out = []
    for l in range(layers):
        centre = current[l]
        low = current[l - 1] if l > 0 else centre
        around = low + pltpu.roll(centre, 1, 0) + pltpu.roll(centre, rows - 1, 0)
        around = around + pltpu.roll(centre, 1, 1) + pltpu.roll(centre, width - 1, 1)
        if l + 1 < len(current):
            around = around + current[l + 1]
        value = centre + CONDUCT_RATE * rates[l] * (around - 6.0 * centre)
        if l == 0 and flux is not None:
            value = value + flux
        out.append(value)
    return out


def rims(low_ref, high_ref, l, width):
    low = lax.broadcasted_iota(jnp.int32, (8, width), 0) < HALO
    before = low_ref[l * 8 : l * 8 + 8].astype(F32)
    after = high_ref[l * 8 : l * 8 + 8].astype(F32)
    return jnp.where(low, after, before), pltpu.roll(jnp.where(low, before, after), HALO, 0)


def liner_kernel(solid_ref, rates_ref, low_ref, high_ref, out_ref, first, second, rates):
    layers, rows, width = solid_ref.shape
    for l in range(layers):
        solid_rim, rates_rim = rims(low_ref, high_ref, l, width)
        first[l, :rows] = solid_ref[l]
        first[l, rows:] = solid_rim
        rates[l, :rows] = CONDUCT_RATE * rates_ref[l]
        rates[l, rows:] = CONDUCT_RATE * rates_rim
    tall = first.shape[1]

    for substep in range(SUBCYCLES):
        source, target = (first, second) if substep % 2 == 0 else (second, first)
        for l in range(layers):
            centre = source[l]
            around = source[max(l - 1, 0)] + pltpu.roll(centre, 1, 0) + pltpu.roll(centre, tall - 1, 0)
            around = around + pltpu.roll(centre, 1, 1) + pltpu.roll(centre, width - 1, 1)
            if l < layers - 1:
                around = around + source[l + 1]
            value = centre + rates[l] * (around - 6.0 * centre)
            if substep == SUBCYCLES - 1:
                out_ref[l] = value[:rows]
            else:
                target[l] = value


def liner(solid, rates, edge_low, edge_high):
    layers, rows, width = solid.shape
    tall = rows + 8
    cells = layers * tall * width
    whole = pl.BlockSpec(solid.shape, lambda i: (0, 0, 0))
    edge = pl.BlockSpec((layers * 8, width), lambda i: (0, 0))
    return pl.pallas_call(
        liner_kernel,
        grid=(1,),
        in_specs=[whole, whole, edge, edge],
        out_specs=whole,
        out_shape=jax.ShapeDtypeStruct(solid.shape, F32),
        scratch_shapes=[pltpu.VMEM((layers, tall, width), F32)] * 3,
        compiler_params=params(),
        cost_estimate=cost(14 * SUBCYCLES * cells, 12 * cells),
        name="liner",
    )(solid, rates, edge_low, edge_high)


def liner_top_kernel(arrived_ref, solid_ref, rates_ref, low_ref, high_ref, rest_ref, out_ref):
    del rest_ref
    depth, rows, width = solid_ref.shape
    mark = rows + HALO - 1
    flux = jnp.zeros(arrived_ref.shape[1:], F32)
    for d in range(arrived_ref.shape[0]):
        part = arrived_ref[d].astype(jnp.int32).astype(F32)
        flux = flux + part * jnp.exp2(part[mark : mark + 1] - 15.0)
    flux = FLUX_GAIN * flux
    current, rates = [], []
    for l in range(depth):
        solid_rim, rates_rim = rims(low_ref, high_ref, l, width)
        current.append(jnp.concatenate([solid_ref[l], solid_rim], axis=0))
        rates.append(jnp.concatenate([rates_ref[l], rates_rim], axis=0))
    for substep in range(SUBCYCLES):
        current = conduct(current, depth - 1 - substep, rates, flux)
    for l in range(SUBCYCLES):
        out_ref[l] = current[l][:rows]


def liner_top(arrived, solid, rates, edge_low, edge_high, rest):
    rows, width = solid.shape[1:]
    depth = 2 * SUBCYCLES
    top = pl.BlockSpec((depth, rows, width), lambda i: (0, 0, 0))
    edge = pl.BlockSpec((depth * 8, width), lambda i: (0, 0))
    cells = depth * (rows + 8) * width
    return pl.pallas_call(
        liner_top_kernel,
        grid=(1,),
        in_specs=[
            pl.BlockSpec(arrived.shape, lambda i: (0, 0, 0)),
            top,
            top,
            edge,
            edge,
            pl.BlockSpec(memory_space=pl.ANY),
        ],
        out_specs=pl.BlockSpec((SUBCYCLES, rows, width), lambda i: (0, 0, 0)),
        out_shape=jax.ShapeDtypeStruct(rest.shape, F32),
        input_output_aliases={5: 0},
        compiler_params=params(),
        cost_estimate=cost(60 * cells, 8 * cells),
        name="liner_top",
    )(arrived, solid, rates, edge_low, edge_high, rest)


def body(
    flow_temp,
    velocity,
    heat_release,
    solid_temp,
    conductivity,
    interp_table,
    flow_patch,
    solid_device,
    solid_patch,
    block_index,
):
    layers, rows, width = flow_temp.shape
    devices = lax.axis_size(AXES)
    up = [(i, (i + 1) % devices) for i in range(devices)]
    down = [(j, i) for i, j in up]

    steps = jnp.round(solid_temp[0] * STEPS_PER_UNIT).astype(I16)
    outgoing = jnp.broadcast_to(steps[None], (devices, rows, width))
    faces = lax.all_to_all(outgoing, AXES, split_axis=0, concat_axis=0, tiled=True)
    faces = faces.reshape(devices * rows, width)

    to_up, to_down = edges(flow_temp, velocity, solid_temp, conductivity)
    before = lax.ppermute(to_up, AXES, up)
    after = lax.ppermute(to_down, AXES, down)

    solid_device = solid_device.reshape(1, -1)
    solid_patch = solid_patch[None]
    flow_p = flow_patch[None]
    weights = weights_of(block_index[None], interp_table.reshape(NODES * NODES, -1))

    mid, mid_first, mid_last = predictor(flow_temp, before, after, velocity, heat_release)
    mid_low = lax.ppermute(mid_last, AXES, up)
    mid_high = lax.ppermute(mid_first, AXES, down)

    wall, wall_first, wall_last = forward(solid_device, solid_patch, flow_p, weights, faces, rows)
    wall_low = lax.ppermute(wall_last, AXES, up)
    wall_high = lax.ppermute(wall_first, AXES, down)

    sending, top, rim = backward(
        solid_device,
        solid_patch,
        flow_p,
        weights,
        wall,
        wall_low,
        wall_high,
        before,
        after,
        mid,
        mid_low,
        mid_high,
        flow_temp,
        velocity,
        heat_release,
        devices,
    )
    arrived = lax.all_to_all(sending, AXES, split_axis=0, concat_axis=0, tiled=True)
    flow_out = corrector(mid, top, wall, rim, mid_low, mid_high, flow_temp, velocity, heat_release)
    rest = liner(solid_temp, conductivity, before, after)
    solid_out = liner_top(arrived, solid_temp, conductivity, before, after, rest)
    return (flow_out, solid_out)


def solution(mesh):
    placed = (
        P(None, AXES, None),
        P(None, None, AXES, None),
        P(None, AXES, None),
        P(None, AXES, None),
        P(None, AXES, None),
        P(),
        P(AXES),
        P(AXES, None),
        P(AXES),
        P(AXES),
    )
    return jax.shard_map(
        body,
        mesh=mesh,
        in_specs=placed,
        out_specs=(P(None, AXES, None), P(None, AXES, None)),
        check_vma=False,
    )
```

```python
import functools

import jax
import jax.numpy as jnp
from jax import lax
from jax.experimental import pallas as pl
from jax.experimental.pallas import tpu as pltpu
from jax.sharding import PartitionSpec as P

SUBCYCLES = 4
DIFFUSION = 0.8
TIMESTEP = 0.12
FILM_COEFF = 1.0
CONDUCT_RATE = 0.08
FLUX_GAIN = 0.25

AXES = ("grp", "dom")
NODES = 16
CHUNK = 2048
WEIGHT_CHUNK = 1024
BLOCK = 64
LANES = 128
LAYERS = 16
HALO = 4
F32 = jnp.float32
BF16 = jnp.bfloat16
VMEM_LIMIT = 58 * 1024 * 1024
STEPS_PER_UNIT = 5461.0
I16 = jnp.int16


def params(**kw):
    return pltpu.CompilerParams(vmem_limit_bytes=VMEM_LIMIT, **kw)


def cost(flops, nbytes):
    return pl.CostEstimate(flops=flops, bytes_accessed=nbytes, transcendentals=0)


def one_hot(index, rows):
    count = index.shape[1]
    wide = jnp.broadcast_to(index, (NODES, count))
    cells = lax.broadcasted_iota(jnp.int32, (NODES, count), 0)
    inner = min(rows, 128)
    low = wide % inner
    high = wide // inner
    parts = [jnp.where(cells + g == low, 1.0, 0.0).astype(BF16) for g in range(0, inner, NODES)]
    out = []
    for h in range(-(-rows // inner)):
        mask = jnp.where(high == h, 1.0, 0.0).astype(BF16)
        out.extend([p * mask for p in parts])
    return jnp.concatenate(out, axis=0)


def dot(a, b):
    return lax.dot_general(a, b, (((1,), (0,)), ((), ())), preferred_element_type=F32)


def dot_nt(a, b):
    return lax.dot_general(a, b, (((1,), (1,)), ((), ())), preferred_element_type=F32)


def split(x):
    high = x.astype(BF16)
    return high, (x - high.astype(F32)).astype(BF16)


def stack(x):
    return jnp.concatenate(split(x), axis=0)


def fold(x):
    half = x.shape[0] // 2
    return x[:half] + x[half:]


def weights_kernel(block_ref, table_ref, out_ref, table):
    @pl.when(pl.program_id(0) == 0)
    def _():
        table[...] = stack(table_ref[...])

    picked = one_hot(block_ref[...], table_ref.shape[1])
    out_ref[...] = fold(dot(table[...], picked))


def weights_of(block_index, table):
    entries, blocks = table.shape
    count = block_index.shape[1]
    return pl.pallas_call(
        weights_kernel,
        grid=(count // WEIGHT_CHUNK,),
        in_specs=[
            pl.BlockSpec((1, WEIGHT_CHUNK), lambda i: (0, i)),
            pl.BlockSpec((entries, blocks), lambda i: (0, 0)),
        ],
        out_specs=pl.BlockSpec((entries, WEIGHT_CHUNK), lambda i: (0, i)),
        out_shape=jax.ShapeDtypeStruct((entries, count), F32),
        scratch_shapes=[pltpu.VMEM((2 * entries, blocks), BF16)],
        compiler_params=params(),
        cost_estimate=cost(4 * entries * blocks * count, 4 * entries * (blocks + count)),
        name="weights",
    )(block_index, table)


def spread_rows(rows_x):
    p = lax.broadcasted_iota(jnp.int32, (rows_x, rows_x * NODES), 1)
    x = lax.broadcasted_iota(jnp.int32, (rows_x, rows_x * NODES), 0)
    return jnp.where(p // NODES == x, 1.0, 0.0).astype(BF16)


def patches_to_face(patches, rows_x):
    count = patches.shape[1]
    c = lax.broadcasted_iota(jnp.int32, (NODES, count), 1) % NODES
    parts = [jnp.where(c == k, patches, 0.0) for k in range(NODES)]
    high, low = split(jnp.concatenate(parts, axis=0))
    rows = spread_rows(rows_x)
    return dot_nt(rows, high) + dot_nt(rows, low)


def face_to_patches(face, rows_x):
    high, low = split(face)
    rows = spread_rows(rows_x)
    wide = lax.dot_general(
        high, rows, (((0,), (0,)), ((), ())), preferred_element_type=F32
    ) + lax.dot_general(low, rows, (((0,), (0,)), ((), ())), preferred_element_type=F32)
    c = lax.broadcasted_iota(jnp.int32, (NODES, rows.shape[1]), 1) % NODES
    out = jnp.zeros((NODES, rows.shape[1]), F32)
    for k in range(NODES):
        out = jnp.where(c == k, wide[k * NODES : (k + 1) * NODES], out)
    return out


def solid_place(device_ref, patch_ref, rows_x):
    per_row = NODES
    patch = patch_ref[...]
    return device_ref[...] * rows_x + patch // per_row, patch % per_row


def forward_kernel(
    device_ref,
    patch_ref,
    flow_p_ref,
    weights_ref,
    faces_ref,
    edge_low_ref,
    edge_high_ref,
    under_ref,
    flow_ref,
    velocity_ref,
    heat_ref,
    wall_ref,
    top_ref,
    first_ref,
    last_ref,
    faces_turned,
    fetched,
    product,
    total,
):
    step = pl.program_id(0)
    rows_x = wall_ref.shape[0]

    @pl.when(step == 0)
    def _():
        faces_turned[...] = stack(faces_ref[...].astype(F32).T)
        total[...] = jnp.zeros_like(total)

    solid_x, solid_c = solid_place(device_ref, patch_ref, rows_x)
    picked = one_hot(solid_x, faces_ref.shape[0])
    fetched[...] = fold(dot(faces_turned[...], picked))
    for k in range(CHUNK // LANES):
        lanes = slice(k * LANES, (k + 1) * LANES)
        c = jnp.broadcast_to(solid_c[:, lanes], (NODES, LANES))
        values = jnp.zeros((NODES, LANES), F32)
        for j in range(NODES):
            values = jnp.where(c == j, fetched[j * NODES : (j + 1) * NODES, lanes], values)
        values = values * (1.0 / STEPS_PER_UNIT)
        for i in range(NODES):
            rows = slice(i * NODES, (i + 1) * NODES)
            high, low = split(weights_ref[rows, lanes] * values)
            product[rows, lanes] = high
            product[NODES * NODES + i * NODES : NODES * NODES + (i + 1) * NODES, lanes] = low
    placed = one_hot(flow_p_ref[...], total.shape[1])
    total[...] += dot_nt(product[...], placed)

    @pl.when(step == pl.num_programs(0) - 1)
    def _():
        patches = jnp.sum(fold(total[...]).reshape(NODES, NODES, total.shape[1]), axis=1)
        wall = patches_to_face(patches, rows_x)
        wall_ref[...] = wall
        edge = edge_low_ref.shape[0]
        lows = edge_low_ref[...].astype(F32)
        highs = edge_high_ref[...].astype(F32)
        for l in range(2):
            centre = flow_ref[l]
            zlow = under_ref[1] if l == 0 else flow_ref[0]
            zhigh = flow_ref[1] if l == 0 else wall
            row = slice(edge - 2 + l, edge - 1 + l)
            xlow, xhigh = x_neighbours(centre, lows[row], highs[row])
            vz, vx, vy = (velocity_ref[d, l].astype(F32) for d in range(3))
            top_ref[l] = centre + TIMESTEP * layer_tendency(
                centre, zlow, zhigh, xlow, xhigh, vz, vx, vy, heat_ref[l].astype(F32)
            )
        first_ref[...] = top_ref[1, :1]
        last_ref[...] = top_ref[1, rows_x - 1 :]


def forward(solid_device, solid_patch, flow_p, weights, faces, edge_low, edge_high, flow, velocity, heat):
    entries, count = weights.shape
    tall, width = faces.shape
    layers, rows_x = flow.shape[:2]
    last = edge_low.shape[0] // LAYERS - 1
    edge = pl.BlockSpec((LAYERS, width), lambda i: (last, 0))
    pair = pl.BlockSpec((2, rows_x, width), lambda i: (layers // 2 - 1, 0, 0))
    line = pl.BlockSpec((1, CHUNK), lambda i: (0, i))
    fixed = lambda shape: pl.BlockSpec(shape, lambda i: (0,) * len(shape))
    return pl.pallas_call(
        forward_kernel,
        grid=(count // CHUNK,),
        in_specs=[
            line,
            line,
            line,
            pl.BlockSpec((entries, CHUNK), lambda i: (0, i)),
            fixed((tall, width)),
            edge,
            edge,
            pl.BlockSpec((2, rows_x, width), lambda i: (layers // 2 - 2, 0, 0)),
            pair,
            pl.BlockSpec((3, 2, rows_x, width), lambda i: (0, layers // 2 - 1, 0, 0)),
            pair,
        ],
        out_specs=[fixed((rows_x, width)), fixed((2, rows_x, width)), fixed((1, width)), fixed((1, width))],
        out_shape=[
            jax.ShapeDtypeStruct((rows_x, width), F32),
            jax.ShapeDtypeStruct((2, rows_x, width), F32),
            jax.ShapeDtypeStruct((1, width), F32),
            jax.ShapeDtypeStruct((1, width), F32),
        ],
        scratch_shapes=[
            pltpu.VMEM((2 * width, tall), BF16),
            pltpu.VMEM((width, CHUNK), F32),
            pltpu.VMEM((2 * entries, CHUNK), BF16),
            pltpu.VMEM((2 * entries, rows_x * NODES), F32),
        ],
        compiler_params=params(),
        cost_estimate=cost(4 * width * (tall + entries) * count, 4 * entries * count),
        name="forward",
    )(solid_device, solid_patch, flow_p, weights, faces, edge_low, edge_high, flow, flow, velocity, heat)


def edges_kernel(
    flow_low_ref, flow_high_ref, solid_ref, rates_ref, up_ref, down_ref
):
    layers = flow_low_ref.shape[0]
    solid_layers, rows, width = solid_ref.shape
    low = lax.broadcasted_iota(jnp.int32, (8, width), 0) < HALO
    for l in range(0, solid_layers, 2):
        ups, downs = [], []
        for m in (l, l + 1):
            ups.append(
                jnp.where(low, pltpu.roll(rates_ref[m, rows - 8 :], HALO, 0), solid_ref[m, rows - 8 :])
            )
            downs.append(jnp.where(low, solid_ref[m, :8], pltpu.roll(rates_ref[m, :8], HALO, 0)))
        up_ref[l * 8 : l * 8 + 16] = jnp.concatenate(ups, axis=0).astype(BF16)
        down_ref[l * 8 : l * 8 + 16] = jnp.concatenate(downs, axis=0).astype(BF16)
    start = solid_layers * 8
    for l in range(0, layers, LAYERS):
        part = slice(start + l, start + l + LAYERS)
        up_ref[part] = jnp.concatenate(
            [flow_high_ref[m, 7:8] for m in range(l, l + LAYERS)], axis=0
        ).astype(BF16)
        down_ref[part] = jnp.concatenate(
            [flow_low_ref[m, 0:1] for m in range(l, l + LAYERS)], axis=0
        ).astype(BF16)


def edges(flow, solid, rates):
    layers, rows, width = flow.shape
    solid_layers = solid.shape[0]
    shape = (solid_layers * 8 + layers, width)
    whole = pl.BlockSpec(solid.shape, lambda i: (0, 0, 0))
    return pl.pallas_call(
        edges_kernel,
        grid=(1,),
        in_specs=[
            pl.BlockSpec((layers, 8, width), lambda i: (0, 0, 0)),
            pl.BlockSpec((layers, 8, width), lambda i: (0, rows // 8 - 1, 0)),
            whole,
            whole,
        ],
        out_specs=[pl.BlockSpec(shape, lambda i: (0, 0))] * 2,
        out_shape=[jax.ShapeDtypeStruct(shape, BF16)] * 2,
        compiler_params=params(),
        cost_estimate=cost(8 * shape[0] * width, 12 * shape[0] * width),
        name="edges",
    )(flow, flow, solid, rates)


def layer_tendency(centre, zlow, zhigh, xlow, xhigh, vz, vx, vy, source):
    width = centre.shape[1]
    total = source
    pairs = (
        (vz, zlow, zhigh),
        (vx, xlow, xhigh),
        (vy, pltpu.roll(centre, 1, 1), pltpu.roll(centre, width - 1, 1)),
    )
    for speed, low, high in pairs:
        a = jnp.maximum(speed, 0.0) + DIFFUSION
        b = a - speed
        total = total + a * (low - centre) + b * (high - centre)
    return total


def x_neighbours(centre, low_row, high_row):
    rows, width = centre.shape
    row = lax.broadcasted_iota(jnp.int32, (rows, width), 0)
    low = jnp.where(row == 0, jnp.broadcast_to(low_row, (rows, width)), pltpu.roll(centre, 1, 0))
    high = jnp.where(
        row == rows - 1, jnp.broadcast_to(high_row, (rows, width)), pltpu.roll(centre, rows - 1, 0)
    )
    return low, high


def predictor_kernel(
    below_ref, flow_ref, above_ref, low_ref, high_ref, velocity_ref, heat_ref, out_ref, first_ref, last_ref
):
    step = pl.program_id(0)
    lows = low_ref[...].astype(F32)
    highs = high_ref[...].astype(F32)
    first, last = [], []
    rows = flow_ref.shape[1]
    for l in range(BLOCK):
        centre = flow_ref[l]
        if l == 0:
            zlow = jnp.where(step == 0, 0.0, below_ref[0])
        else:
            zlow = flow_ref[l - 1]
        if l == BLOCK - 1:
            zhigh = jnp.where(step == pl.num_programs(0) - 1, 0.0, above_ref[0])
        else:
            zhigh = flow_ref[l + 1]
        xlow, xhigh = x_neighbours(centre, lows[l : l + 1], highs[l : l + 1])
        vz, vx, vy = (velocity_ref[d, l].astype(F32) for d in range(3))
        value = centre + TIMESTEP * layer_tendency(
            centre, zlow, zhigh, xlow, xhigh, vz, vx, vy, heat_ref[l].astype(F32)
        )
        out_ref[l] = value
        first.append(value[0:1])
        last.append(value[rows - 1 : rows])
    first_ref[...] = jnp.concatenate(first, axis=0).astype(BF16)
    last_ref[...] = jnp.concatenate(last, axis=0).astype(BF16)


def layer_specs(shape, halo=True):
    layers, rows, width = shape
    block = pl.BlockSpec((BLOCK, rows, width), lambda i: (i, 0, 0))
    below = pl.BlockSpec((1, rows, width), lambda i: (jnp.maximum(i * BLOCK - 1, 0), 0, 0))
    above = pl.BlockSpec((1, rows, width), lambda i: (jnp.minimum((i + 1) * BLOCK, layers - 1), 0, 0))
    speeds = pl.BlockSpec((3, BLOCK, rows, width), lambda i: (0, i, 0, 0))
    edge = pl.BlockSpec((BLOCK, width), lambda i: (i, 0))
    return block, below, above, speeds, edge


def predictor(flow, low, high, velocity, heat):
    layers, rows, width = flow.shape
    block, below, above, speeds, edge = layer_specs(flow.shape)
    cells = layers * rows * width
    first_edge = (low.shape[0] - layers) // BLOCK
    flow_edge = pl.BlockSpec((BLOCK, width), lambda i: (i + first_edge, 0))
    return pl.pallas_call(
        predictor_kernel,
        grid=(layers // BLOCK,),
        in_specs=[below, block, above, flow_edge, flow_edge, speeds, block],
        out_specs=[block, edge, edge],
        out_shape=[
            jax.ShapeDtypeStruct(flow.shape, F32),
            jax.ShapeDtypeStruct((layers, width), BF16),
            jax.ShapeDtypeStruct((layers, width), BF16),
        ],
        compiler_params=params(),
        cost_estimate=cost(40 * cells, 16 * cells),
        name="predictor",
    )(flow, flow, flow, low, high, velocity, heat)


def corrector_kernel(
    below_ref,
    mid_ref,
    above_ref,
    top_ref,
    wall_ref,
    top_low_ref,
    top_high_ref,
    low_ref,
    high_ref,
    flow_ref,
    velocity_ref,
    heat_ref,
    out_ref,
):
    step = pl.program_id(0)
    final = step == pl.num_programs(0) - 1
    lows = low_ref[...].astype(F32)
    highs = high_ref[...].astype(F32)
    for l in range(BLOCK):
        centre = mid_ref[l]
        low_row, high_row = lows[l : l + 1], highs[l : l + 1]
        zlow = jnp.where(step == 0, 0.0, below_ref[0]) if l == 0 else mid_ref[l - 1]
        if l == BLOCK - 1:
            centre = jnp.where(final, top_ref[1], centre)
            zhigh = jnp.where(final, wall_ref[...], above_ref[0])
            low_row = jnp.where(final, top_low_ref[...], low_row)
            high_row = jnp.where(final, top_high_ref[...], high_row)
        elif l == BLOCK - 2:
            zhigh = jnp.where(final, top_ref[1], mid_ref[l + 1])
        else:
            zhigh = mid_ref[l + 1]
        xlow, xhigh = x_neighbours(centre, low_row, high_row)
        vz, vx, vy = (velocity_ref[d, l].astype(F32) for d in range(3))
        slope = layer_tendency(centre, zlow, zhigh, xlow, xhigh, vz, vx, vy, heat_ref[l].astype(F32))
        out_ref[l] = 0.5 * flow_ref[l] + 0.5 * (centre + TIMESTEP * slope)


def corrector(mid, top, wall, top_low, top_high, low, high, flow, velocity, heat):
    layers, rows, width = flow.shape
    block, below, above, speeds, edge = layer_specs(flow.shape)
    face = pl.BlockSpec((rows, width), lambda i: (0, 0))
    line = pl.BlockSpec((1, width), lambda i: (0, 0))
    cells = layers * rows * width
    return pl.pallas_call(
        corrector_kernel,
        grid=(layers // BLOCK,),
        in_specs=[below, block, above, pl.BlockSpec(top.shape, lambda i: (0, 0, 0)), face, line, line, edge, edge, block, speeds, block],
        out_specs=block,
        out_shape=jax.ShapeDtypeStruct(flow.shape, F32),
        compiler_params=params(),
        cost_estimate=cost(44 * cells, 20 * cells),
        name="corrector",
    )(mid, mid, mid, top, wall, top_low, top_high, low, high, flow, velocity, heat)


def backward_kernel(
    device_ref,
    patch_ref,
    flow_p_ref,
    weights_ref,
    wall_ref,
    top_ref,
    low_ref,
    high_ref,
    flow_ref,
    velocity_ref,
    heat_ref,
    send_ref,
    flux_high,
    flux_low,
    fetched,
    returned_high,
    returned_low,
    total,
):
    step = pl.program_id(0)
    rows, width = wall_ref.shape

    @pl.when(step == 0)
    def _():
        total[...] = jnp.zeros_like(total)
        wall = wall_ref[...]
        vz, vx, vy = (velocity_ref[d, 0].astype(F32) for d in range(3))
        top = top_ref[1]
        xlow, xhigh = x_neighbours(top, low_ref[...], high_ref[...])
        slope = layer_tendency(top, top_ref[0], wall, xlow, xhigh, vz, vx, vy, heat_ref[0].astype(F32))
        out = 0.5 * flow_ref[0] + 0.5 * (top + TIMESTEP * slope)
        patches = face_to_patches(FILM_COEFF * (out - wall), rows)
        wide = jnp.broadcast_to(patches[:, None, :], (NODES, NODES, patches.shape[1]))
        high, low = split(wide.reshape(NODES * NODES, patches.shape[1]))
        flux_high[...] = high
        flux_low[...] = low

    picked = one_hot(flow_p_ref[...], flux_high.shape[1])
    fetched[...] = dot(flux_high[...], picked) + dot(flux_low[...], picked)
    solid_x, solid_c = solid_place(device_ref, patch_ref, rows)
    for k in range(CHUNK // LANES):
        lanes = slice(k * LANES, (k + 1) * LANES)
        value = jnp.zeros((NODES, LANES), F32)
        for i in range(NODES):
            part = slice(i * NODES, (i + 1) * NODES)
            value = value + weights_ref[part, lanes] * fetched[part, lanes]
        c = jnp.broadcast_to(solid_c[:, lanes], (NODES, LANES))
        high, low = split(value)
        high, low = high.astype(F32), low.astype(F32)
        for j in range(NODES):
            part = slice(j * NODES, (j + 1) * NODES)
            returned_high[part, lanes] = jnp.where(c == j, high, 0.0).astype(BF16)
            returned_low[part, lanes] = jnp.where(c == j, low, 0.0).astype(BF16)
    placed = one_hot(solid_x, total.shape[0])
    total[...] += dot_nt(placed, returned_high[...]) + dot_nt(placed, returned_low[...])

    @pl.when(step == pl.num_programs(0) - 1)
    def _():
        devices = send_ref.shape[0]
        tall = total.shape[0]
        peak = jnp.zeros((8, width), F32)
        for r in range(0, tall, 8):
            peak = jnp.maximum(peak, jnp.abs(total[r : r + 8]))
        peak = jnp.maximum(jnp.max(peak, axis=0, keepdims=True), 1e-30)
        power = jnp.floor(jnp.log2(peak)) + 1.0
        factor = jnp.exp2(15.0 - power)
        sub = lax.broadcasted_iota(jnp.int32, (8, width), 0)
        for d in range(devices):
            own = total[d * rows : (d + 1) * rows]
            after = ((d + 1) * rows) % tall
            before = (d * rows - 8) % tall
            rim = jnp.where(sub < HALO, total[after : after + 8], total[before : before + 8])
            scaled = jnp.clip(jnp.round(jnp.concatenate([own, rim], axis=0) * factor), -32767.0, 32767.0)
            place = lax.broadcasted_iota(jnp.int32, scaled.shape, 0) == rows + HALO - 1
            scaled = jnp.where(place, jnp.broadcast_to(power, scaled.shape), scaled)
            send_ref[d] = scaled.astype(jnp.int32).astype(I16)


def backward(solid_device, solid_patch, flow_p, weights, wall, top, low, high, flow, velocity, heat, devices):
    entries, count = weights.shape
    rows, width = wall.shape
    layers = flow.shape[0]
    tall = devices * rows
    line = pl.BlockSpec((1, CHUNK), lambda i: (0, i))
    fixed = lambda shape: pl.BlockSpec(shape, lambda i: (0,) * len(shape))
    return pl.pallas_call(
        backward_kernel,
        grid=(count // CHUNK,),
        in_specs=[
            line,
            line,
            line,
            pl.BlockSpec((entries, CHUNK), lambda i: (0, i)),
            fixed((rows, width)),
            fixed((2, rows, width)),
            fixed((1, width)),
            fixed((1, width)),
            pl.BlockSpec((1, rows, width), lambda i: (layers - 1, 0, 0)),
            pl.BlockSpec((3, 1, rows, width), lambda i: (0, layers - 1, 0, 0)),
            pl.BlockSpec((1, rows, width), lambda i: (layers - 1, 0, 0)),
        ],
        out_specs=fixed((devices, rows + 8, width)),
        out_shape=jax.ShapeDtypeStruct((devices, rows + 8, width), I16),
        scratch_shapes=[
            pltpu.VMEM((entries, rows * NODES), BF16),
            pltpu.VMEM((entries, rows * NODES), BF16),
            pltpu.VMEM((entries, CHUNK), F32),
            pltpu.VMEM((width, CHUNK), BF16),
            pltpu.VMEM((width, CHUNK), BF16),
            pltpu.VMEM((tall, width), F32),
        ],
        compiler_params=params(),
        cost_estimate=cost(4 * width * (tall + entries) * count, 4 * entries * count),
        name="backward",
    )(solid_device, solid_patch, flow_p, weights, wall, top, low, high, flow, velocity, heat)


def conduct(current, layers, rates, flux):
    rows = current[0].shape[0]
    width = current[0].shape[1]
    out = []
    for l in range(layers):
        centre = current[l]
        low = current[l - 1] if l > 0 else centre
        around = low + pltpu.roll(centre, 1, 0) + pltpu.roll(centre, rows - 1, 0)
        around = around + pltpu.roll(centre, 1, 1) + pltpu.roll(centre, width - 1, 1)
        if l + 1 < len(current):
            around = around + current[l + 1]
        value = centre + CONDUCT_RATE * rates[l] * (around - 6.0 * centre)
        if l == 0 and flux is not None:
            value = value + flux
        out.append(value)
    return out


def rims(low_ref, high_ref, l, width):
    low = lax.broadcasted_iota(jnp.int32, (8, width), 0) < HALO
    before = low_ref[l * 8 : l * 8 + 8].astype(F32)
    after = high_ref[l * 8 : l * 8 + 8].astype(F32)
    return jnp.where(low, after, before), pltpu.roll(jnp.where(low, before, after), HALO, 0)


def liner_kernel(solid_ref, rates_ref, low_ref, high_ref, out_ref, first, second, rates):
    layers, rows, width = solid_ref.shape
    for l in range(layers):
        solid_rim, rates_rim = rims(low_ref, high_ref, l, width)
        first[l, :rows] = solid_ref[l]
        first[l, rows:] = solid_rim
        rates[l, :rows] = CONDUCT_RATE * rates_ref[l]
        rates[l, rows:] = CONDUCT_RATE * rates_rim
    tall = first.shape[1]

    for substep in range(SUBCYCLES):
        source, target = (first, second) if substep % 2 == 0 else (second, first)
        for l in range(layers):
            centre = source[l]
            around = source[max(l - 1, 0)] + pltpu.roll(centre, 1, 0) + pltpu.roll(centre, tall - 1, 0)
            around = around + pltpu.roll(centre, 1, 1) + pltpu.roll(centre, width - 1, 1)
            if l < layers - 1:
                around = around + source[l + 1]
            value = centre + rates[l] * (around - 6.0 * centre)
            if substep == SUBCYCLES - 1:
                out_ref[l] = value[:rows]
            else:
                target[l] = value


def liner(solid, rates, edge_low, edge_high):
    layers, rows, width = solid.shape
    tall = rows + 8
    cells = layers * tall * width
    whole = pl.BlockSpec(solid.shape, lambda i: (0, 0, 0))
    edge = pl.BlockSpec((layers * 8, width), lambda i: (0, 0))
    return pl.pallas_call(
        liner_kernel,
        grid=(1,),
        in_specs=[whole, whole, edge, edge],
        out_specs=whole,
        out_shape=jax.ShapeDtypeStruct(solid.shape, F32),
        scratch_shapes=[pltpu.VMEM((layers, tall, width), F32)] * 3,
        compiler_params=params(),
        cost_estimate=cost(14 * SUBCYCLES * cells, 12 * cells),
        name="liner",
    )(solid, rates, edge_low, edge_high)


def liner_top_kernel(arrived_ref, solid_ref, rates_ref, low_ref, high_ref, rest_ref, out_ref):
    del rest_ref
    depth, rows, width = solid_ref.shape
    mark = rows + HALO - 1
    flux = jnp.zeros(arrived_ref.shape[1:], F32)
    for d in range(arrived_ref.shape[0]):
        part = arrived_ref[d].astype(jnp.int32).astype(F32)
        flux = flux + part * jnp.exp2(part[mark : mark + 1] - 15.0)
    flux = FLUX_GAIN * flux
    current, rates = [], []
    for l in range(depth):
        solid_rim, rates_rim = rims(low_ref, high_ref, l, width)
        current.append(jnp.concatenate([solid_ref[l], solid_rim], axis=0))
        rates.append(jnp.concatenate([rates_ref[l], rates_rim], axis=0))
    for substep in range(SUBCYCLES):
        current = conduct(current, depth - 1 - substep, rates, flux)
    for l in range(SUBCYCLES):
        out_ref[l] = current[l][:rows]


def liner_top(arrived, solid, rates, edge_low, edge_high, rest):
    rows, width = solid.shape[1:]
    depth = 2 * SUBCYCLES
    top = pl.BlockSpec((depth, rows, width), lambda i: (0, 0, 0))
    edge = pl.BlockSpec((depth * 8, width), lambda i: (0, 0))
    cells = depth * (rows + 8) * width
    return pl.pallas_call(
        liner_top_kernel,
        grid=(1,),
        in_specs=[
            pl.BlockSpec(arrived.shape, lambda i: (0, 0, 0)),
            top,
            top,
            edge,
            edge,
            pl.BlockSpec(memory_space=pl.ANY),
        ],
        out_specs=pl.BlockSpec((SUBCYCLES, rows, width), lambda i: (0, 0, 0)),
        out_shape=jax.ShapeDtypeStruct(rest.shape, F32),
        input_output_aliases={5: 0},
        compiler_params=params(),
        cost_estimate=cost(60 * cells, 8 * cells),
        name="liner_top",
    )(arrived, solid, rates, edge_low, edge_high, rest)


def body(
    flow_temp,
    velocity,
    heat_release,
    solid_temp,
    conductivity,
    interp_table,
    flow_patch,
    solid_device,
    solid_patch,
    block_index,
):
    layers, rows, width = flow_temp.shape
    devices = lax.axis_size(AXES)
    up = [(i, (i + 1) % devices) for i in range(devices)]
    down = [(j, i) for i, j in up]

    steps = jnp.round(solid_temp[0] * STEPS_PER_UNIT).astype(I16)
    outgoing = jnp.broadcast_to(steps[None], (devices, rows, width))
    faces = lax.all_to_all(outgoing, AXES, split_axis=0, concat_axis=0, tiled=True)
    faces = faces.reshape(devices * rows, width)

    to_up, to_down = edges(flow_temp, solid_temp, conductivity)
    before = lax.ppermute(to_up, AXES, up)
    after = lax.ppermute(to_down, AXES, down)

    solid_device = solid_device.reshape(1, -1)
    solid_patch = solid_patch[None]
    flow_p = flow_patch[None]
    weights = weights_of(block_index[None], interp_table.reshape(NODES * NODES, -1))

    wall, top, top_first, top_last = forward(
        solid_device, solid_patch, flow_p, weights, faces, before, after, flow_temp, velocity, heat_release
    )
    top_low = lax.ppermute(top_last, AXES, up)
    top_high = lax.ppermute(top_first, AXES, down)

    before, after, wall = lax.optimization_barrier((before, after, wall))
    mid, mid_first, mid_last = predictor(flow_temp, before, after, velocity, heat_release)
    mid_low = lax.ppermute(mid_last, AXES, up)
    mid_high = lax.ppermute(mid_first, AXES, down)
    top_low, top_high, mid_first = lax.optimization_barrier((top_low, top_high, mid_first))

    sending = backward(
        solid_device,
        solid_patch,
        flow_p,
        weights,
        wall,
        top,
        top_low,
        top_high,
        flow_temp,
        velocity,
        heat_release,
        devices,
    )
    sending, top, before = lax.optimization_barrier((sending, top, before))
    arrived = lax.all_to_all(sending, AXES, split_axis=0, concat_axis=0, tiled=True)
    flow_out = corrector(
        mid, top, wall, top_low, top_high, mid_low, mid_high, flow_temp, velocity, heat_release
    )
    rest = liner(solid_temp, conductivity, before, after)
    solid_out = liner_top(arrived, solid_temp, conductivity, before, after, rest)
    return (flow_out, solid_out)


def solution(mesh):
    placed = (
        P(None, AXES, None),
        P(None, None, AXES, None),
        P(None, AXES, None),
        P(None, AXES, None),
        P(None, AXES, None),
        P(),
        P(AXES),
        P(AXES, None),
        P(AXES),
        P(AXES),
    )
    return jax.shard_map(
        body,
        mesh=mesh,
        in_specs=placed,
        out_specs=(P(None, AXES, None), P(None, AXES, None)),
        check_vma=False,
    )
```

```python
import functools

import jax
import jax.numpy as jnp
from jax import lax
from jax.experimental import pallas as pl
from jax.experimental.pallas import tpu as pltpu
from jax.sharding import PartitionSpec as P

SUBCYCLES = 4
DIFFUSION = 0.8
TIMESTEP = 0.12
FILM_COEFF = 1.0
CONDUCT_RATE = 0.08
FLUX_GAIN = 0.25

AXES = ("grp", "dom")
NODES = 16
CHUNK = 2048
WEIGHT_CHUNK = 1024
BLOCK = 64
LANES = 128
LAYERS = 16
HALO = 4
F32 = jnp.float32
BF16 = jnp.bfloat16
VMEM_LIMIT = 63 * 1000 * 1000
STEPS_PER_UNIT = 5461.0
I16 = jnp.int16


def params(**kw):
    return pltpu.CompilerParams(vmem_limit_bytes=VMEM_LIMIT, **kw)


def cost(flops, nbytes):
    return pl.CostEstimate(flops=flops, bytes_accessed=nbytes, transcendentals=0)


def one_hot(index, rows):
    cells = lax.broadcasted_iota(jnp.int16, (rows, index.shape[1]), 0)
    return jnp.where(cells == index.astype(jnp.int16), BF16(1), BF16(0))


def dot(a, b):
    return lax.dot_general(a, b, (((1,), (0,)), ((), ())), preferred_element_type=F32)


def dot_nt(a, b):
    return lax.dot_general(a, b, (((1,), (1,)), ((), ())), preferred_element_type=F32)


def sides(pair, cross):
    even = lax.axis_index(AXES[1]) % 2 == 0
    return jnp.where(even, cross, pair), jnp.where(even, pair, cross)


def lots(to_before, to_after):
    even = lax.axis_index(AXES[1]) % 2 == 0
    return jnp.where(even, to_after, to_before), jnp.where(even, to_before, to_after)


def split(x):
    high = x.astype(BF16)
    return high, (x - high.astype(F32)).astype(BF16)


def stack(x):
    return jnp.concatenate(split(x), axis=0)


def fold(x):
    half = x.shape[0] // 2
    return x[:half] + x[half:]


def weights_kernel(block_ref, table_ref, out_ref, table):
    @pl.when(pl.program_id(0) == 0)
    def _():
        table[...] = stack(table_ref[...])

    picked = one_hot(block_ref[...], table_ref.shape[1])
    out_ref[...] = fold(dot(table[...], picked))


def weights_of(block_index, table):
    entries, blocks = table.shape
    count = block_index.shape[1]
    return pl.pallas_call(
        weights_kernel,
        grid=(count // WEIGHT_CHUNK,),
        in_specs=[
            pl.BlockSpec((1, WEIGHT_CHUNK), lambda i: (0, i)),
            pl.BlockSpec((entries, blocks), lambda i: (0, 0)),
        ],
        out_specs=pl.BlockSpec((entries, WEIGHT_CHUNK), lambda i: (0, i)),
        out_shape=jax.ShapeDtypeStruct((entries, count), F32),
        scratch_shapes=[pltpu.VMEM((2 * entries, blocks), BF16)],
        compiler_params=params(),
        cost_estimate=cost(4 * entries * blocks * count, 4 * entries * (blocks + count)),
        name="weights",
    )(block_index, table)


def spread_rows(rows_x):
    p = lax.broadcasted_iota(jnp.int32, (rows_x, rows_x * NODES), 1)
    x = lax.broadcasted_iota(jnp.int32, (rows_x, rows_x * NODES), 0)
    return jnp.where(p // NODES == x, 1.0, 0.0).astype(BF16)


def patches_to_face(patches, rows_x):
    count = patches.shape[1]
    c = lax.broadcasted_iota(jnp.int32, (NODES, count), 1) % NODES
    parts = [jnp.where(c == k, patches, 0.0) for k in range(NODES)]
    high, low = split(jnp.concatenate(parts, axis=0))
    rows = spread_rows(rows_x)
    return dot_nt(rows, high) + dot_nt(rows, low)


def face_to_patches(face, rows_x):
    high, low = split(face)
    rows = spread_rows(rows_x)
    wide = lax.dot_general(
        high, rows, (((0,), (0,)), ((), ())), preferred_element_type=F32
    ) + lax.dot_general(low, rows, (((0,), (0,)), ((), ())), preferred_element_type=F32)
    c = lax.broadcasted_iota(jnp.int32, (NODES, rows.shape[1]), 1) % NODES
    out = jnp.zeros((NODES, rows.shape[1]), F32)
    for k in range(NODES):
        out = jnp.where(c == k, wide[k * NODES : (k + 1) * NODES], out)
    return out


def solid_place(device_ref, patch_ref, rows_x):
    per_row = NODES
    patch = patch_ref[...]
    return device_ref[...] * rows_x + patch // per_row, patch % per_row


def forward_kernel(
    device_ref,
    patch_ref,
    flow_p_ref,
    weights_ref,
    faces_ref,
    edge_pair_ref,
    edge_cross_ref,
    under_ref,
    flow_ref,
    velocity_ref,
    heat_ref,
    wall_ref,
    top_ref,
    first_ref,
    last_ref,
    faces_turned,
    fetched,
    product,
    total,
):
    step = pl.program_id(0)
    rows_x = wall_ref.shape[0]

    @pl.when(step == 0)
    def _():
        faces_turned[...] = stack(faces_ref[...].astype(F32).T)
        total[...] = jnp.zeros_like(total)

    solid_x, solid_c = solid_place(device_ref, patch_ref, rows_x)
    picked = one_hot(solid_x, faces_ref.shape[0])
    fetched[...] = fold(dot(faces_turned[...], picked))
    for k in range(CHUNK // LANES):
        lanes = slice(k * LANES, (k + 1) * LANES)
        c = jnp.broadcast_to(solid_c[:, lanes], (NODES, LANES))
        values = jnp.zeros((NODES, LANES), F32)
        for j in range(NODES):
            values = jnp.where(c == j, fetched[j * NODES : (j + 1) * NODES, lanes], values)
        values = values * (1.0 / STEPS_PER_UNIT)
        for i in range(NODES):
            rows = slice(i * NODES, (i + 1) * NODES)
            high, low = split(weights_ref[rows, lanes] * values)
            product[rows, lanes] = high
            product[NODES * NODES + i * NODES : NODES * NODES + (i + 1) * NODES, lanes] = low
    placed = one_hot(flow_p_ref[...], total.shape[1])
    total[...] += dot_nt(product[...], placed)

    @pl.when(step == pl.num_programs(0) - 1)
    def _():
        patches = jnp.sum(fold(total[...]).reshape(NODES, NODES, total.shape[1]), axis=1)
        wall = patches_to_face(patches, rows_x)
        wall_ref[...] = wall
        edge = edge_pair_ref.shape[0]
        lows, highs = sides(edge_pair_ref[...].astype(F32), edge_cross_ref[...].astype(F32))
        for l in range(2):
            centre = flow_ref[l]
            zlow = under_ref[1] if l == 0 else flow_ref[0]
            zhigh = flow_ref[1] if l == 0 else wall
            row = slice(edge - 2 + l, edge - 1 + l)
            xlow, xhigh = x_neighbours(centre, lows[row], highs[row])
            vz, vx, vy = (velocity_ref[d, l].astype(F32) for d in range(3))
            top_ref[l] = centre + TIMESTEP * layer_tendency(
                centre, zlow, zhigh, xlow, xhigh, vz, vx, vy, heat_ref[l].astype(F32)
            )
        first_ref[...], last_ref[...] = lots(top_ref[1, :1], top_ref[1, rows_x - 1 :])


def forward(solid_device, solid_patch, flow_p, weights, faces, edge_pair, edge_cross, flow, velocity, heat):
    entries, count = weights.shape
    tall, width = faces.shape
    layers, rows_x = flow.shape[:2]
    last = edge_pair.shape[0] // LAYERS - 1
    edge = pl.BlockSpec((LAYERS, width), lambda i: (last, 0))
    pair = pl.BlockSpec((2, rows_x, width), lambda i: (layers // 2 - 1, 0, 0))
    line = pl.BlockSpec((1, CHUNK), lambda i: (0, i))
    fixed = lambda shape: pl.BlockSpec(shape, lambda i: (0,) * len(shape))
    return pl.pallas_call(
        forward_kernel,
        grid=(count // CHUNK,),
        in_specs=[
            line,
            line,
            line,
            pl.BlockSpec((entries, CHUNK), lambda i: (0, i)),
            fixed((tall, width)),
            edge,
            edge,
            pl.BlockSpec((2, rows_x, width), lambda i: (layers // 2 - 2, 0, 0)),
            pair,
            pl.BlockSpec((3, 2, rows_x, width), lambda i: (0, layers // 2 - 1, 0, 0)),
            pair,
        ],
        out_specs=[fixed((rows_x, width)), fixed((2, rows_x, width)), fixed((1, width)), fixed((1, width))],
        out_shape=[
            jax.ShapeDtypeStruct((rows_x, width), F32),
            jax.ShapeDtypeStruct((2, rows_x, width), F32),
            jax.ShapeDtypeStruct((1, width), F32),
            jax.ShapeDtypeStruct((1, width), F32),
        ],
        scratch_shapes=[
            pltpu.VMEM((2 * width, tall), BF16),
            pltpu.VMEM((width, CHUNK), F32),
            pltpu.VMEM((2 * entries, CHUNK), BF16),
            pltpu.VMEM((2 * entries, rows_x * NODES), F32),
        ],
        compiler_params=params(),
        cost_estimate=cost(4 * width * (tall + entries) * count, 4 * entries * count),
        name="forward",
    )(solid_device, solid_patch, flow_p, weights, faces, edge_pair, edge_cross, flow, flow, velocity, heat)


def edges_kernel(
    flow_low_ref, flow_high_ref, solid_ref, rates_ref, pair_ref, cross_ref
):
    layers = flow_low_ref.shape[0]
    solid_layers, rows, width = solid_ref.shape
    low = lax.broadcasted_iota(jnp.int32, (8, width), 0) < HALO
    for l in range(0, solid_layers, 2):
        ups, downs = [], []
        for m in (l, l + 1):
            ups.append(
                jnp.where(low, pltpu.roll(rates_ref[m, rows - 8 :], HALO, 0), solid_ref[m, rows - 8 :])
            )
            downs.append(jnp.where(low, solid_ref[m, :8], pltpu.roll(rates_ref[m, :8], HALO, 0)))
        pair, cross = lots(jnp.concatenate(downs, axis=0), jnp.concatenate(ups, axis=0))
        pair_ref[l * 8 : l * 8 + 16] = pair.astype(BF16)
        cross_ref[l * 8 : l * 8 + 16] = cross.astype(BF16)
    start = solid_layers * 8
    for l in range(0, layers, LAYERS):
        part = slice(start + l, start + l + LAYERS)
        pair, cross = lots(
            jnp.concatenate([flow_low_ref[m, 0:1] for m in range(l, l + LAYERS)], axis=0),
            jnp.concatenate([flow_high_ref[m, 7:8] for m in range(l, l + LAYERS)], axis=0),
        )
        pair_ref[part] = pair.astype(BF16)
        cross_ref[part] = cross.astype(BF16)


def edges(flow, solid, rates):
    layers, rows, width = flow.shape
    solid_layers = solid.shape[0]
    shape = (solid_layers * 8 + layers, width)
    whole = pl.BlockSpec(solid.shape, lambda i: (0, 0, 0))
    return pl.pallas_call(
        edges_kernel,
        grid=(1,),
        in_specs=[
            pl.BlockSpec((layers, 8, width), lambda i: (0, 0, 0)),
            pl.BlockSpec((layers, 8, width), lambda i: (0, rows // 8 - 1, 0)),
            whole,
            whole,
        ],
        out_specs=[pl.BlockSpec(shape, lambda i: (0, 0))] * 2,
        out_shape=[jax.ShapeDtypeStruct(shape, BF16)] * 2,
        compiler_params=params(),
        cost_estimate=cost(8 * shape[0] * width, 12 * shape[0] * width),
        name="edges",
    )(flow, flow, solid, rates)


def layer_tendency(centre, zlow, zhigh, xlow, xhigh, vz, vx, vy, source):
    width = centre.shape[1]
    total = source
    pairs = (
        (vz, zlow, zhigh),
        (vx, xlow, xhigh),
        (vy, pltpu.roll(centre, 1, 1), pltpu.roll(centre, width - 1, 1)),
    )
    for speed, low, high in pairs:
        a = jnp.maximum(speed, 0.0) + DIFFUSION
        b = a - speed
        total = total + a * (low - centre) + b * (high - centre)
    return total


def x_neighbours(centre, low_row, high_row):
    rows, width = centre.shape
    row = lax.broadcasted_iota(jnp.int32, (rows, width), 0)
    low = jnp.where(row == 0, jnp.broadcast_to(low_row, (rows, width)), pltpu.roll(centre, 1, 0))
    high = jnp.where(
        row == rows - 1, jnp.broadcast_to(high_row, (rows, width)), pltpu.roll(centre, rows - 1, 0)
    )
    return low, high


def predictor_kernel(
    below_ref, flow_ref, above_ref, pair_ref, cross_ref, velocity_ref, heat_ref, out_ref, first_ref, last_ref
):
    step = pl.program_id(0)
    lows, highs = sides(pair_ref[...].astype(F32), cross_ref[...].astype(F32))
    first, last = [], []
    rows = flow_ref.shape[1]
    for l in range(BLOCK):
        centre = flow_ref[l]
        if l == 0:
            zlow = jnp.where(step == 0, 0.0, below_ref[0])
        else:
            zlow = flow_ref[l - 1]
        if l == BLOCK - 1:
            zhigh = jnp.where(step == pl.num_programs(0) - 1, 0.0, above_ref[0])
        else:
            zhigh = flow_ref[l + 1]
        xlow, xhigh = x_neighbours(centre, lows[l : l + 1], highs[l : l + 1])
        vz, vx, vy = (velocity_ref[d, l].astype(F32) for d in range(3))
        value = centre + TIMESTEP * layer_tendency(
            centre, zlow, zhigh, xlow, xhigh, vz, vx, vy, heat_ref[l].astype(F32)
        )
        out_ref[l] = value
        first.append(value[0:1])
        last.append(value[rows - 1 : rows])
    pair, cross = lots(jnp.concatenate(first, axis=0), jnp.concatenate(last, axis=0))
    first_ref[...] = pair.astype(BF16)
    last_ref[...] = cross.astype(BF16)


def layer_specs(shape, halo=True):
    layers, rows, width = shape
    block = pl.BlockSpec((BLOCK, rows, width), lambda i: (i, 0, 0))
    below = pl.BlockSpec((1, rows, width), lambda i: (jnp.maximum(i * BLOCK - 1, 0), 0, 0))
    above = pl.BlockSpec((1, rows, width), lambda i: (jnp.minimum((i + 1) * BLOCK, layers - 1), 0, 0))
    speeds = pl.BlockSpec((3, BLOCK, rows, width), lambda i: (0, i, 0, 0))
    edge = pl.BlockSpec((BLOCK, width), lambda i: (i, 0))
    return block, below, above, speeds, edge


def predictor(flow, low, high, velocity, heat):
    layers, rows, width = flow.shape
    block, below, above, speeds, edge = layer_specs(flow.shape)
    cells = layers * rows * width
    first_edge = (low.shape[0] - layers) // BLOCK
    flow_edge = pl.BlockSpec((BLOCK, width), lambda i: (i + first_edge, 0))
    return pl.pallas_call(
        predictor_kernel,
        grid=(layers // BLOCK,),
        in_specs=[below, block, above, flow_edge, flow_edge, speeds, block],
        out_specs=[block, edge, edge],
        out_shape=[
            jax.ShapeDtypeStruct(flow.shape, F32),
            jax.ShapeDtypeStruct((layers, width), BF16),
            jax.ShapeDtypeStruct((layers, width), BF16),
        ],
        compiler_params=params(),
        cost_estimate=cost(40 * cells, 16 * cells),
        name="predictor",
    )(flow, flow, flow, low, high, velocity, heat)


def corrector_kernel(
    below_ref,
    mid_ref,
    above_ref,
    top_ref,
    wall_ref,
    top_pair_ref,
    top_cross_ref,
    pair_ref,
    cross_ref,
    flow_ref,
    velocity_ref,
    heat_ref,
    out_ref,
):
    step = pl.program_id(0)
    final = step == pl.num_programs(0) - 1
    lows, highs = sides(pair_ref[...].astype(F32), cross_ref[...].astype(F32))
    for l in range(BLOCK):
        centre = mid_ref[l]
        low_row, high_row = lows[l : l + 1], highs[l : l + 1]
        zlow = jnp.where(step == 0, 0.0, below_ref[0]) if l == 0 else mid_ref[l - 1]
        if l == BLOCK - 1:
            centre = jnp.where(final, top_ref[1], centre)
            zhigh = jnp.where(final, wall_ref[...], above_ref[0])
            top_low, top_high = sides(top_pair_ref[...], top_cross_ref[...])
            low_row = jnp.where(final, top_low, low_row)
            high_row = jnp.where(final, top_high, high_row)
        elif l == BLOCK - 2:
            zhigh = jnp.where(final, top_ref[1], mid_ref[l + 1])
        else:
            zhigh = mid_ref[l + 1]
        xlow, xhigh = x_neighbours(centre, low_row, high_row)
        vz, vx, vy = (velocity_ref[d, l].astype(F32) for d in range(3))
        slope = layer_tendency(centre, zlow, zhigh, xlow, xhigh, vz, vx, vy, heat_ref[l].astype(F32))
        out_ref[l] = 0.5 * flow_ref[l] + 0.5 * (centre + TIMESTEP * slope)


def corrector(mid, top, wall, top_low, top_high, low, high, flow, velocity, heat):
    layers, rows, width = flow.shape
    block, below, above, speeds, edge = layer_specs(flow.shape)
    face = pl.BlockSpec((rows, width), lambda i: (0, 0))
    line = pl.BlockSpec((1, width), lambda i: (0, 0))
    cells = layers * rows * width
    return pl.pallas_call(
        corrector_kernel,
        grid=(layers // BLOCK,),
        in_specs=[below, block, above, pl.BlockSpec(top.shape, lambda i: (0, 0, 0)), face, line, line, edge, edge, block, speeds, block],
        out_specs=block,
        out_shape=jax.ShapeDtypeStruct(flow.shape, F32),
        compiler_params=params(),
        cost_estimate=cost(44 * cells, 20 * cells),
        name="corrector",
    )(mid, mid, mid, top, wall, top_low, top_high, low, high, flow, velocity, heat)


def backward_kernel(
    device_ref,
    patch_ref,
    flow_p_ref,
    weights_ref,
    wall_ref,
    top_ref,
    pair_ref,
    cross_ref,
    flow_ref,
    velocity_ref,
    heat_ref,
    send_ref,
    flux_high,
    flux_low,
    fetched,
    returned_high,
    returned_low,
    total,
):
    step = pl.program_id(0)
    rows, width = wall_ref.shape

    @pl.when(step == 0)
    def _():
        total[...] = jnp.zeros_like(total)
        wall = wall_ref[...]
        vz, vx, vy = (velocity_ref[d, 0].astype(F32) for d in range(3))
        top = top_ref[1]
        xlow, xhigh = x_neighbours(top, *sides(pair_ref[...], cross_ref[...]))
        slope = layer_tendency(top, top_ref[0], wall, xlow, xhigh, vz, vx, vy, heat_ref[0].astype(F32))
        out = 0.5 * flow_ref[0] + 0.5 * (top + TIMESTEP * slope)
        patches = face_to_patches(FILM_COEFF * (out - wall), rows)
        wide = jnp.broadcast_to(patches[:, None, :], (NODES, NODES, patches.shape[1]))
        high, low = split(wide.reshape(NODES * NODES, patches.shape[1]))
        flux_high[...] = high
        flux_low[...] = low

    picked = one_hot(flow_p_ref[...], flux_high.shape[1])
    fetched[...] = dot(flux_high[...], picked) + dot(flux_low[...], picked)
    solid_x, solid_c = solid_place(device_ref, patch_ref, rows)
    for k in range(CHUNK // LANES):
        lanes = slice(k * LANES, (k + 1) * LANES)
        value = jnp.zeros((NODES, LANES), F32)
        for i in range(NODES):
            part = slice(i * NODES, (i + 1) * NODES)
            value = value + weights_ref[part, lanes] * fetched[part, lanes]
        c = jnp.broadcast_to(solid_c[:, lanes], (NODES, LANES))
        high, low = split(value)
        high, low = high.astype(F32), low.astype(F32)
        for j in range(NODES):
            part = slice(j * NODES, (j + 1) * NODES)
            returned_high[part, lanes] = jnp.where(c == j, high, 0.0).astype(BF16)
            returned_low[part, lanes] = jnp.where(c == j, low, 0.0).astype(BF16)
    placed = one_hot(solid_x, total.shape[0])
    total[...] += dot_nt(placed, returned_high[...]) + dot_nt(placed, returned_low[...])

    @pl.when(step == pl.num_programs(0) - 1)
    def _():
        devices = send_ref.shape[0]
        tall = total.shape[0]
        peak = jnp.zeros((8, width), F32)
        for r in range(0, tall, 8):
            peak = jnp.maximum(peak, jnp.abs(total[r : r + 8]))
        peak = jnp.maximum(jnp.max(peak, axis=0, keepdims=True), 1e-30)
        power = jnp.floor(jnp.log2(peak)) + 1.0
        factor = jnp.exp2(15.0 - power)
        sub = lax.broadcasted_iota(jnp.int32, (8, width), 0)
        for d in range(devices):
            own = total[d * rows : (d + 1) * rows]
            after = ((d + 1) * rows) % tall
            before = (d * rows - 8) % tall
            rim = jnp.where(sub < HALO, total[after : after + 8], total[before : before + 8])
            scaled = jnp.clip(jnp.round(jnp.concatenate([own, rim], axis=0) * factor), -32767.0, 32767.0)
            place = lax.broadcasted_iota(jnp.int32, scaled.shape, 0) == rows + HALO - 1
            scaled = jnp.where(place, jnp.broadcast_to(power, scaled.shape), scaled)
            send_ref[d] = scaled.astype(jnp.int32).astype(I16)


def backward(solid_device, solid_patch, flow_p, weights, wall, top, low, high, flow, velocity, heat, devices):
    entries, count = weights.shape
    rows, width = wall.shape
    layers = flow.shape[0]
    tall = devices * rows
    line = pl.BlockSpec((1, CHUNK), lambda i: (0, i))
    fixed = lambda shape: pl.BlockSpec(shape, lambda i: (0,) * len(shape))
    return pl.pallas_call(
        backward_kernel,
        grid=(count // CHUNK,),
        in_specs=[
            line,
            line,
            line,
            pl.BlockSpec((entries, CHUNK), lambda i: (0, i)),
            fixed((rows, width)),
            fixed((2, rows, width)),
            fixed((1, width)),
            fixed((1, width)),
            pl.BlockSpec((1, rows, width), lambda i: (layers - 1, 0, 0)),
            pl.BlockSpec((3, 1, rows, width), lambda i: (0, layers - 1, 0, 0)),
            pl.BlockSpec((1, rows, width), lambda i: (layers - 1, 0, 0)),
        ],
        out_specs=fixed((devices, rows + 8, width)),
        out_shape=jax.ShapeDtypeStruct((devices, rows + 8, width), I16),
        scratch_shapes=[
            pltpu.VMEM((entries, rows * NODES), BF16),
            pltpu.VMEM((entries, rows * NODES), BF16),
            pltpu.VMEM((entries, CHUNK), F32),
            pltpu.VMEM((width, CHUNK), BF16),
            pltpu.VMEM((width, CHUNK), BF16),
            pltpu.VMEM((tall, width), F32),
        ],
        compiler_params=params(),
        cost_estimate=cost(4 * width * (tall + entries) * count, 4 * entries * count),
        name="backward",
    )(solid_device, solid_patch, flow_p, weights, wall, top, low, high, flow, velocity, heat)


def conduct(current, layers, rates, flux):
    rows = current[0].shape[0]
    width = current[0].shape[1]
    out = []
    for l in range(layers):
        centre = current[l]
        low = current[l - 1] if l > 0 else centre
        around = low + pltpu.roll(centre, 1, 0) + pltpu.roll(centre, rows - 1, 0)
        around = around + pltpu.roll(centre, 1, 1) + pltpu.roll(centre, width - 1, 1)
        if l + 1 < len(current):
            around = around + current[l + 1]
        value = centre + CONDUCT_RATE * rates[l] * (around - 6.0 * centre)
        if l == 0 and flux is not None:
            value = value + flux
        out.append(value)
    return out


def rims(pair_ref, cross_ref, l, width):
    low = lax.broadcasted_iota(jnp.int32, (8, width), 0) < HALO
    part = slice(l * 8, l * 8 + 8)
    before, after = sides(pair_ref[part].astype(F32), cross_ref[part].astype(F32))
    return jnp.where(low, after, before), pltpu.roll(jnp.where(low, before, after), HALO, 0)


def liner_kernel(solid_ref, rates_ref, pair_ref, cross_ref, out_ref, first, second, rates):
    layers, rows, width = solid_ref.shape
    for l in range(layers):
        solid_rim, rates_rim = rims(pair_ref, cross_ref, l, width)
        first[l, :rows] = solid_ref[l]
        first[l, rows:] = solid_rim
        rates[l, :rows] = CONDUCT_RATE * rates_ref[l]
        rates[l, rows:] = CONDUCT_RATE * rates_rim
    tall = first.shape[1]

    for substep in range(SUBCYCLES):
        source, target = (first, second) if substep % 2 == 0 else (second, first)
        for l in range(layers):
            centre = source[l]
            around = source[max(l - 1, 0)] + pltpu.roll(centre, 1, 0) + pltpu.roll(centre, tall - 1, 0)
            around = around + pltpu.roll(centre, 1, 1) + pltpu.roll(centre, width - 1, 1)
            if l < layers - 1:
                around = around + source[l + 1]
            value = centre + rates[l] * (around - 6.0 * centre)
            if substep == SUBCYCLES - 1:
                out_ref[l] = value[:rows]
            else:
                target[l] = value


def liner(solid, rates, edge_pair, edge_cross):
    layers, rows, width = solid.shape
    tall = rows + 8
    cells = layers * tall * width
    whole = pl.BlockSpec(solid.shape, lambda i: (0, 0, 0))
    edge = pl.BlockSpec((layers * 8, width), lambda i: (0, 0))
    return pl.pallas_call(
        liner_kernel,
        grid=(1,),
        in_specs=[whole, whole, edge, edge],
        out_specs=whole,
        out_shape=jax.ShapeDtypeStruct(solid.shape, F32),
        scratch_shapes=[pltpu.VMEM((layers, tall, width), F32)] * 3,
        compiler_params=params(),
        cost_estimate=cost(14 * SUBCYCLES * cells, 12 * cells),
        name="liner",
    )(solid, rates, edge_pair, edge_cross)


def liner_top_kernel(arrived_ref, solid_ref, rates_ref, pair_ref, cross_ref, rest_ref, out_ref):
    del rest_ref
    depth, rows, width = solid_ref.shape
    mark = rows + HALO - 1
    flux = jnp.zeros(arrived_ref.shape[1:], F32)
    for d in range(arrived_ref.shape[0]):
        part = arrived_ref[d].astype(jnp.int32).astype(F32)
        flux = flux + part * jnp.exp2(part[mark : mark + 1] - 15.0)
    flux = FLUX_GAIN * flux
    current, rates = [], []
    for l in range(depth):
        solid_rim, rates_rim = rims(pair_ref, cross_ref, l, width)
        current.append(jnp.concatenate([solid_ref[l], solid_rim], axis=0))
        rates.append(jnp.concatenate([rates_ref[l], rates_rim], axis=0))
    for substep in range(SUBCYCLES):
        current = conduct(current, depth - 1 - substep, rates, flux)
    for l in range(SUBCYCLES):
        out_ref[l] = current[l][:rows]


def liner_top(arrived, solid, rates, edge_pair, edge_cross, rest):
    rows, width = solid.shape[1:]
    depth = 2 * SUBCYCLES
    top = pl.BlockSpec((depth, rows, width), lambda i: (0, 0, 0))
    edge = pl.BlockSpec((depth * 8, width), lambda i: (0, 0))
    cells = depth * (rows + 8) * width
    return pl.pallas_call(
        liner_top_kernel,
        grid=(1,),
        in_specs=[
            pl.BlockSpec(arrived.shape, lambda i: (0, 0, 0)),
            top,
            top,
            edge,
            edge,
            pl.BlockSpec(memory_space=pl.ANY),
        ],
        out_specs=pl.BlockSpec((SUBCYCLES, rows, width), lambda i: (0, 0, 0)),
        out_shape=jax.ShapeDtypeStruct(rest.shape, F32),
        input_output_aliases={5: 0},
        compiler_params=params(),
        cost_estimate=cost(60 * cells, 8 * cells),
        name="liner_top",
    )(arrived, solid, rates, edge_pair, edge_cross, rest)


def body(
    flow_temp,
    velocity,
    heat_release,
    solid_temp,
    conductivity,
    interp_table,
    flow_patch,
    solid_device,
    solid_patch,
    block_index,
):
    layers, rows, width = flow_temp.shape
    devices = lax.axis_size(AXES)
    near = [(i, i + 1 if i % 2 == 0 else i - 1) for i in range(devices)]
    far = [(i, (i - 1 if i % 2 == 0 else i + 1) % devices) for i in range(devices)]

    steps = jnp.round(solid_temp[0] * STEPS_PER_UNIT).astype(I16)
    outgoing = jnp.broadcast_to(steps[None], (devices, rows, width))
    faces = lax.all_to_all(outgoing, AXES, split_axis=0, concat_axis=0, tiled=True)
    faces = faces.reshape(devices * rows, width)

    to_pair, to_cross = edges(flow_temp, solid_temp, conductivity)
    pair = lax.ppermute(to_pair, AXES, near)
    cross = lax.ppermute(to_cross, AXES, far)

    solid_device = solid_device.reshape(1, -1)
    solid_patch = solid_patch[None]
    flow_p = flow_patch[None]
    weights = weights_of(block_index[None], interp_table.reshape(NODES * NODES, -1))

    wall, top, to_top_pair, to_top_cross = forward(
        solid_device, solid_patch, flow_p, weights, faces, pair, cross, flow_temp, velocity, heat_release
    )
    top_pair = lax.ppermute(to_top_pair, AXES, near)
    top_cross = lax.ppermute(to_top_cross, AXES, far)

    pair, cross, wall = lax.optimization_barrier((pair, cross, wall))
    mid, to_mid_pair, to_mid_cross = predictor(flow_temp, pair, cross, velocity, heat_release)
    mid_pair = lax.ppermute(to_mid_pair, AXES, near)
    mid_cross = lax.ppermute(to_mid_cross, AXES, far)
    top_pair, top_cross, to_mid_pair = lax.optimization_barrier((top_pair, top_cross, to_mid_pair))

    sending = backward(
        solid_device,
        solid_patch,
        flow_p,
        weights,
        wall,
        top,
        top_pair,
        top_cross,
        flow_temp,
        velocity,
        heat_release,
        devices,
    )
    sending, top, pair, mid_pair, mid_cross = lax.optimization_barrier(
        (sending, top, pair, mid_pair, mid_cross)
    )
    arrived = lax.all_to_all(sending, AXES, split_axis=0, concat_axis=0, tiled=True)
    flow_out = corrector(
        mid, top, wall, top_pair, top_cross, mid_pair, mid_cross, flow_temp, velocity, heat_release
    )
    rest = liner(solid_temp, conductivity, pair, cross)
    solid_out = liner_top(arrived, solid_temp, conductivity, pair, cross, rest)
    return (flow_out, solid_out)


def solution(mesh):
    placed = (
        P(None, AXES, None),
        P(None, None, AXES, None),
        P(None, AXES, None),
        P(None, AXES, None),
        P(None, AXES, None),
        P(),
        P(AXES),
        P(AXES, None),
        P(AXES),
        P(AXES),
    )
    return jax.shard_map(
        body,
        mesh=mesh,
        in_specs=placed,
        out_specs=(P(None, AXES, None), P(None, AXES, None)),
        check_vma=False,
    )
```

```python
import functools

import jax
import jax.numpy as jnp
from jax import lax
from jax.experimental import pallas as pl
from jax.experimental.pallas import tpu as pltpu
from jax.sharding import PartitionSpec as P

SUBCYCLES = 4
DIFFUSION = 0.8
TIMESTEP = 0.12
FILM_COEFF = 1.0
CONDUCT_RATE = 0.08
FLUX_GAIN = 0.25

AXES = ("grp", "dom")
NODES = 16
CHUNK = 2048
WEIGHT_CHUNK = 1024
BLOCK = 64
LANES = 128
LAYERS = 16
HALO = 4
F32 = jnp.float32
BF16 = jnp.bfloat16
VMEM_LIMIT = 63 * 1000 * 1000
STEPS_PER_UNIT = 5461.0
I16 = jnp.int16


def params(limit=VMEM_LIMIT):
    return pltpu.CompilerParams(vmem_limit_bytes=limit)


def cost(flops, nbytes):
    return pl.CostEstimate(flops=flops, bytes_accessed=nbytes, transcendentals=0)


def one_hot(index, rows):
    cells = lax.broadcasted_iota(jnp.int16, (rows, index.shape[1]), 0)
    return jnp.where(cells == index.astype(jnp.int16), BF16(1), BF16(0))


def dot(a, b):
    return lax.dot_general(a, b, (((1,), (0,)), ((), ())), preferred_element_type=F32)


def dot_nt(a, b):
    return lax.dot_general(a, b, (((1,), (1,)), ((), ())), preferred_element_type=F32)


def sides(pair, cross):
    even = lax.axis_index(AXES[1]) % 2 == 0
    return jnp.where(even, cross, pair), jnp.where(even, pair, cross)


def lots(to_before, to_after):
    even = lax.axis_index(AXES[1]) % 2 == 0
    return jnp.where(even, to_after, to_before), jnp.where(even, to_before, to_after)


def split(x):
    high = x.astype(BF16)
    return high, (x - high.astype(F32)).astype(BF16)


def stack(x):
    return jnp.concatenate(split(x), axis=0)


def fold(x):
    half = x.shape[0] // 2
    return x[:half] + x[half:]


def weights_kernel(block_ref, table_ref, out_ref, table):
    @pl.when(pl.program_id(0) == 0)
    def _():
        table[...] = stack(table_ref[...])

    picked = one_hot(block_ref[...], table_ref.shape[1])
    out_ref[...] = fold(dot(table[...], picked))


def weights_of(block_index, table):
    entries, blocks = table.shape
    count = block_index.shape[1]
    return pl.pallas_call(
        weights_kernel,
        grid=(count // WEIGHT_CHUNK,),
        in_specs=[
            pl.BlockSpec((1, WEIGHT_CHUNK), lambda i: (0, i)),
            pl.BlockSpec((entries, blocks), lambda i: (0, 0)),
        ],
        out_specs=pl.BlockSpec((entries, WEIGHT_CHUNK), lambda i: (0, i)),
        out_shape=jax.ShapeDtypeStruct((entries, count), F32),
        scratch_shapes=[pltpu.VMEM((2 * entries, blocks), BF16)],
        compiler_params=params(),
        cost_estimate=cost(4 * entries * blocks * count, 4 * entries * (blocks + count)),
        name="weights",
    )(block_index, table)


def spread_rows(rows_x):
    p = lax.broadcasted_iota(jnp.int32, (rows_x, rows_x * NODES), 1)
    x = lax.broadcasted_iota(jnp.int32, (rows_x, rows_x * NODES), 0)
    return jnp.where(p // NODES == x, 1.0, 0.0).astype(BF16)


def patches_to_face(patches, rows_x):
    count = patches.shape[1]
    c = lax.broadcasted_iota(jnp.int32, (NODES, count), 1) % NODES
    parts = [jnp.where(c == k, patches, 0.0) for k in range(NODES)]
    high, low = split(jnp.concatenate(parts, axis=0))
    rows = spread_rows(rows_x)
    return dot_nt(rows, high) + dot_nt(rows, low)


def face_to_patches(face, rows_x):
    high, low = split(face)
    rows = spread_rows(rows_x)
    wide = lax.dot_general(
        high, rows, (((0,), (0,)), ((), ())), preferred_element_type=F32
    ) + lax.dot_general(low, rows, (((0,), (0,)), ((), ())), preferred_element_type=F32)
    c = lax.broadcasted_iota(jnp.int32, (NODES, rows.shape[1]), 1) % NODES
    out = jnp.zeros((NODES, rows.shape[1]), F32)
    for k in range(NODES):
        out = jnp.where(c == k, wide[k * NODES : (k + 1) * NODES], out)
    return out


def solid_place(device_ref, patch_ref, rows_x):
    per_row = NODES
    patch = patch_ref[...]
    return device_ref[...] * rows_x + patch // per_row, patch % per_row


def forward_kernel(
    device_ref,
    patch_ref,
    flow_p_ref,
    weights_ref,
    faces_ref,
    edge_pair_ref,
    edge_cross_ref,
    under_ref,
    flow_ref,
    velocity_ref,
    heat_ref,
    wall_ref,
    top_ref,
    first_ref,
    last_ref,
    faces_turned,
    fetched,
    product,
    total,
):
    step = pl.program_id(0)
    rows_x = wall_ref.shape[0]

    @pl.when(step == 0)
    def _():
        faces_turned[...] = stack(faces_ref[...].astype(F32).T)
        total[...] = jnp.zeros_like(total)

    solid_x, solid_c = solid_place(device_ref, patch_ref, rows_x)
    picked = one_hot(solid_x, faces_ref.shape[0])
    fetched[...] = fold(dot(faces_turned[...], picked))
    for k in range(CHUNK // LANES):
        lanes = slice(k * LANES, (k + 1) * LANES)
        c = jnp.broadcast_to(solid_c[:, lanes], (NODES, LANES))
        values = jnp.zeros((NODES, LANES), F32)
        for j in range(NODES):
            values = jnp.where(c == j, fetched[j * NODES : (j + 1) * NODES, lanes], values)
        values = values * (1.0 / STEPS_PER_UNIT)
        for i in range(NODES):
            rows = slice(i * NODES, (i + 1) * NODES)
            high, low = split(weights_ref[rows, lanes] * values)
            product[rows, lanes] = high
            product[NODES * NODES + i * NODES : NODES * NODES + (i + 1) * NODES, lanes] = low
    placed = one_hot(flow_p_ref[...], total.shape[1])
    total[...] += dot_nt(product[...], placed)

    @pl.when(step == pl.num_programs(0) - 1)
    def _():
        patches = jnp.sum(fold(total[...]).reshape(NODES, NODES, total.shape[1]), axis=1)
        wall = patches_to_face(patches, rows_x)
        wall_ref[...] = wall
        edge = edge_pair_ref.shape[0]
        lows, highs = sides(edge_pair_ref[...].astype(F32), edge_cross_ref[...].astype(F32))
        for l in range(2):
            centre = flow_ref[l]
            zlow = under_ref[1] if l == 0 else flow_ref[0]
            zhigh = flow_ref[1] if l == 0 else wall
            row = slice(edge - 2 + l, edge - 1 + l)
            xlow, xhigh = x_neighbours(centre, lows[row], highs[row])
            vz, vx, vy = (velocity_ref[d, l].astype(F32) for d in range(3))
            top_ref[l] = centre + TIMESTEP * layer_tendency(
                centre, zlow, zhigh, xlow, xhigh, vz, vx, vy, heat_ref[l].astype(F32)
            )
        first_ref[...], last_ref[...] = lots(top_ref[1, :1], top_ref[1, rows_x - 1 :])


def forward(solid_device, solid_patch, flow_p, weights, faces, edge_pair, edge_cross, flow, velocity, heat):
    entries, count = weights.shape
    tall, width = faces.shape
    layers, rows_x = flow.shape[:2]
    last = edge_pair.shape[0] // LAYERS - 1
    edge = pl.BlockSpec((LAYERS, width), lambda i: (last, 0))
    pair = pl.BlockSpec((2, rows_x, width), lambda i: (layers // 2 - 1, 0, 0))
    line = pl.BlockSpec((1, CHUNK), lambda i: (0, i))
    fixed = lambda shape: pl.BlockSpec(shape, lambda i: (0,) * len(shape))
    return pl.pallas_call(
        forward_kernel,
        grid=(count // CHUNK,),
        in_specs=[
            line,
            line,
            line,
            pl.BlockSpec((entries, CHUNK), lambda i: (0, i)),
            fixed((tall, width)),
            edge,
            edge,
            pl.BlockSpec((2, rows_x, width), lambda i: (layers // 2 - 2, 0, 0)),
            pair,
            pl.BlockSpec((3, 2, rows_x, width), lambda i: (0, layers // 2 - 1, 0, 0)),
            pair,
        ],
        out_specs=[fixed((rows_x, width)), fixed((2, rows_x, width)), fixed((1, width)), fixed((1, width))],
        out_shape=[
            jax.ShapeDtypeStruct((rows_x, width), F32),
            jax.ShapeDtypeStruct((2, rows_x, width), F32),
            jax.ShapeDtypeStruct((1, width), F32),
            jax.ShapeDtypeStruct((1, width), F32),
        ],
        scratch_shapes=[
            pltpu.VMEM((2 * width, tall), BF16),
            pltpu.VMEM((width, CHUNK), F32),
            pltpu.VMEM((2 * entries, CHUNK), BF16),
            pltpu.VMEM((2 * entries, rows_x * NODES), F32),
        ],
        compiler_params=params(),
        cost_estimate=cost(4 * width * (tall + entries) * count, 4 * entries * count),
        name="forward",
    )(solid_device, solid_patch, flow_p, weights, faces, edge_pair, edge_cross, flow, flow, velocity, heat)


def edges_kernel(
    flow_low_ref, flow_high_ref, solid_ref, rates_ref, pair_ref, cross_ref
):
    layers = flow_low_ref.shape[0]
    solid_layers, rows, width = solid_ref.shape
    low = lax.broadcasted_iota(jnp.int32, (8, width), 0) < HALO
    for l in range(0, solid_layers, 2):
        ups, downs = [], []
        for m in (l, l + 1):
            ups.append(
                jnp.where(low, pltpu.roll(rates_ref[m, rows - 8 :], HALO, 0), solid_ref[m, rows - 8 :])
            )
            downs.append(jnp.where(low, solid_ref[m, :8], pltpu.roll(rates_ref[m, :8], HALO, 0)))
        pair, cross = lots(jnp.concatenate(downs, axis=0), jnp.concatenate(ups, axis=0))
        pair_ref[l * 8 : l * 8 + 16] = pair.astype(BF16)
        cross_ref[l * 8 : l * 8 + 16] = cross.astype(BF16)
    start = solid_layers * 8
    for l in range(0, layers, LAYERS):
        part = slice(start + l, start + l + LAYERS)
        pair, cross = lots(
            jnp.concatenate([flow_low_ref[m, 0:1] for m in range(l, l + LAYERS)], axis=0),
            jnp.concatenate([flow_high_ref[m, 7:8] for m in range(l, l + LAYERS)], axis=0),
        )
        pair_ref[part] = pair.astype(BF16)
        cross_ref[part] = cross.astype(BF16)


def edges(flow, solid, rates):
    layers, rows, width = flow.shape
    solid_layers = solid.shape[0]
    shape = (solid_layers * 8 + layers, width)
    whole = pl.BlockSpec(solid.shape, lambda i: (0, 0, 0))
    return pl.pallas_call(
        edges_kernel,
        grid=(1,),
        in_specs=[
            pl.BlockSpec((layers, 8, width), lambda i: (0, 0, 0)),
            pl.BlockSpec((layers, 8, width), lambda i: (0, rows // 8 - 1, 0)),
            whole,
            whole,
        ],
        out_specs=[pl.BlockSpec(shape, lambda i: (0, 0))] * 2,
        out_shape=[jax.ShapeDtypeStruct(shape, BF16)] * 2,
        compiler_params=params(),
        cost_estimate=cost(8 * shape[0] * width, 12 * shape[0] * width),
        name="edges",
    )(flow, flow, solid, rates)


def layer_tendency(centre, zlow, zhigh, xlow, xhigh, vz, vx, vy, source):
    width = centre.shape[1]
    total = source
    pairs = (
        (vz, zlow, zhigh),
        (vx, xlow, xhigh),
        (vy, pltpu.roll(centre, 1, 1), pltpu.roll(centre, width - 1, 1)),
    )
    for speed, low, high in pairs:
        a = jnp.maximum(speed, 0.0) + DIFFUSION
        b = a - speed
        total = total + a * (low - centre) + b * (high - centre)
    return total


def x_neighbours(centre, low_row, high_row):
    rows, width = centre.shape
    row = lax.broadcasted_iota(jnp.int32, (rows, width), 0)
    low = jnp.where(row == 0, jnp.broadcast_to(low_row, (rows, width)), pltpu.roll(centre, 1, 0))
    high = jnp.where(
        row == rows - 1, jnp.broadcast_to(high_row, (rows, width)), pltpu.roll(centre, rows - 1, 0)
    )
    return low, high


def predictor_kernel(
    below_ref, flow_ref, above_ref, pair_ref, cross_ref, velocity_ref, heat_ref, out_ref, first_ref, last_ref
):
    step = pl.program_id(0)
    lows, highs = sides(pair_ref[...].astype(F32), cross_ref[...].astype(F32))
    first, last = [], []
    rows = flow_ref.shape[1]
    for l in range(BLOCK):
        centre = flow_ref[l]
        if l == 0:
            zlow = jnp.where(step == 0, 0.0, below_ref[0])
        else:
            zlow = flow_ref[l - 1]
        if l == BLOCK - 1:
            zhigh = jnp.where(step == pl.num_programs(0) - 1, 0.0, above_ref[0])
        else:
            zhigh = flow_ref[l + 1]
        xlow, xhigh = x_neighbours(centre, lows[l : l + 1], highs[l : l + 1])
        vz, vx, vy = (velocity_ref[d, l].astype(F32) for d in range(3))
        value = centre + TIMESTEP * layer_tendency(
            centre, zlow, zhigh, xlow, xhigh, vz, vx, vy, heat_ref[l].astype(F32)
        )
        out_ref[l] = value
        first.append(value[0:1])
        last.append(value[rows - 1 : rows])
    pair, cross = lots(jnp.concatenate(first, axis=0), jnp.concatenate(last, axis=0))
    first_ref[...] = pair.astype(BF16)
    last_ref[...] = cross.astype(BF16)


def layer_specs(shape, halo=True):
    layers, rows, width = shape
    block = pl.BlockSpec((BLOCK, rows, width), lambda i: (i, 0, 0))
    below = pl.BlockSpec((1, rows, width), lambda i: (jnp.maximum(i * BLOCK - 1, 0), 0, 0))
    above = pl.BlockSpec((1, rows, width), lambda i: (jnp.minimum((i + 1) * BLOCK, layers - 1), 0, 0))
    speeds = pl.BlockSpec((3, BLOCK, rows, width), lambda i: (0, i, 0, 0))
    edge = pl.BlockSpec((BLOCK, width), lambda i: (i, 0))
    return block, below, above, speeds, edge


def predictor(flow, low, high, velocity, heat):
    layers, rows, width = flow.shape
    block, below, above, speeds, edge = layer_specs(flow.shape)
    cells = layers * rows * width
    first_edge = (low.shape[0] - layers) // BLOCK
    flow_edge = pl.BlockSpec((BLOCK, width), lambda i: (i + first_edge, 0))
    return pl.pallas_call(
        predictor_kernel,
        grid=(layers // BLOCK,),
        in_specs=[below, block, above, flow_edge, flow_edge, speeds, block],
        out_specs=[block, edge, edge],
        out_shape=[
            jax.ShapeDtypeStruct(flow.shape, F32),
            jax.ShapeDtypeStruct((layers, width), BF16),
            jax.ShapeDtypeStruct((layers, width), BF16),
        ],
        compiler_params=params(),
        cost_estimate=cost(40 * cells, 16 * cells),
        name="predictor",
    )(flow, flow, flow, low, high, velocity, heat)


def corrector_kernel(
    below_ref,
    mid_ref,
    above_ref,
    top_ref,
    wall_ref,
    top_pair_ref,
    top_cross_ref,
    pair_ref,
    cross_ref,
    flow_ref,
    velocity_ref,
    heat_ref,
    out_ref,
):
    step = pl.program_id(0)
    final = step == pl.num_programs(0) - 1
    lows, highs = sides(pair_ref[...].astype(F32), cross_ref[...].astype(F32))
    for l in range(BLOCK):
        centre = mid_ref[l]
        low_row, high_row = lows[l : l + 1], highs[l : l + 1]
        zlow = jnp.where(step == 0, 0.0, below_ref[0]) if l == 0 else mid_ref[l - 1]
        if l == BLOCK - 1:
            centre = jnp.where(final, top_ref[1], centre)
            zhigh = jnp.where(final, wall_ref[...], above_ref[0])
            top_low, top_high = sides(top_pair_ref[...], top_cross_ref[...])
            low_row = jnp.where(final, top_low, low_row)
            high_row = jnp.where(final, top_high, high_row)
        elif l == BLOCK - 2:
            zhigh = jnp.where(final, top_ref[1], mid_ref[l + 1])
        else:
            zhigh = mid_ref[l + 1]
        xlow, xhigh = x_neighbours(centre, low_row, high_row)
        vz, vx, vy = (velocity_ref[d, l].astype(F32) for d in range(3))
        slope = layer_tendency(centre, zlow, zhigh, xlow, xhigh, vz, vx, vy, heat_ref[l].astype(F32))
        out_ref[l] = 0.5 * flow_ref[l] + 0.5 * (centre + TIMESTEP * slope)


def corrector(mid, top, wall, top_low, top_high, low, high, flow, velocity, heat):
    layers, rows, width = flow.shape
    block, below, above, speeds, edge = layer_specs(flow.shape)
    face = pl.BlockSpec((rows, width), lambda i: (0, 0))
    line = pl.BlockSpec((1, width), lambda i: (0, 0))
    cells = layers * rows * width
    return pl.pallas_call(
        corrector_kernel,
        grid=(layers // BLOCK,),
        in_specs=[below, block, above, pl.BlockSpec(top.shape, lambda i: (0, 0, 0)), face, line, line, edge, edge, block, speeds, block],
        out_specs=block,
        out_shape=jax.ShapeDtypeStruct(flow.shape, F32),
        compiler_params=params(),
        cost_estimate=cost(44 * cells, 20 * cells),
        name="corrector",
    )(mid, mid, mid, top, wall, top_low, top_high, low, high, flow, velocity, heat)


def backward_kernel(
    device_ref,
    patch_ref,
    flow_p_ref,
    weights_ref,
    wall_ref,
    top_ref,
    pair_ref,
    cross_ref,
    flow_ref,
    velocity_ref,
    heat_ref,
    send_ref,
    flux_high,
    flux_low,
    fetched,
    returned_high,
    returned_low,
    total,
):
    step = pl.program_id(0)
    rows, width = wall_ref.shape

    @pl.when(step == 0)
    def _():
        total[...] = jnp.zeros_like(total)
        wall = wall_ref[...]
        vz, vx, vy = (velocity_ref[d, 0].astype(F32) for d in range(3))
        top = top_ref[1]
        xlow, xhigh = x_neighbours(top, *sides(pair_ref[...], cross_ref[...]))
        slope = layer_tendency(top, top_ref[0], wall, xlow, xhigh, vz, vx, vy, heat_ref[0].astype(F32))
        out = 0.5 * flow_ref[0] + 0.5 * (top + TIMESTEP * slope)
        patches = face_to_patches(FILM_COEFF * (out - wall), rows)
        wide = jnp.broadcast_to(patches[:, None, :], (NODES, NODES, patches.shape[1]))
        high, low = split(wide.reshape(NODES * NODES, patches.shape[1]))
        flux_high[...] = high
        flux_low[...] = low

    picked = one_hot(flow_p_ref[...], flux_high.shape[1])
    fetched[...] = dot(flux_high[...], picked) + dot(flux_low[...], picked)
    solid_x, solid_c = solid_place(device_ref, patch_ref, rows)
    for k in range(CHUNK // LANES):
        lanes = slice(k * LANES, (k + 1) * LANES)
        value = jnp.zeros((NODES, LANES), F32)
        for i in range(NODES):
            part = slice(i * NODES, (i + 1) * NODES)
            value = value + weights_ref[part, lanes] * fetched[part, lanes]
        c = jnp.broadcast_to(solid_c[:, lanes], (NODES, LANES))
        high, low = split(value)
        high, low = high.astype(F32), low.astype(F32)
        for j in range(NODES):
            part = slice(j * NODES, (j + 1) * NODES)
            returned_high[part, lanes] = jnp.where(c == j, high, 0.0).astype(BF16)
            returned_low[part, lanes] = jnp.where(c == j, low, 0.0).astype(BF16)
    placed = one_hot(solid_x, total.shape[0])
    total[...] += dot_nt(placed, returned_high[...]) + dot_nt(placed, returned_low[...])

    @pl.when(step == pl.num_programs(0) - 1)
    def _():
        devices = send_ref.shape[0]
        tall = total.shape[0]
        peak = jnp.zeros((8, width), F32)
        for r in range(0, tall, 8):
            peak = jnp.maximum(peak, jnp.abs(total[r : r + 8]))
        peak = jnp.maximum(jnp.max(peak, axis=0, keepdims=True), 1e-30)
        power = jnp.floor(jnp.log2(peak)) + 1.0
        factor = jnp.exp2(15.0 - power)
        sub = lax.broadcasted_iota(jnp.int32, (8, width), 0)
        for d in range(devices):
            own = total[d * rows : (d + 1) * rows]
            after = ((d + 1) * rows) % tall
            before = (d * rows - 8) % tall
            rim = jnp.where(sub < HALO, total[after : after + 8], total[before : before + 8])
            scaled = jnp.clip(jnp.round(jnp.concatenate([own, rim], axis=0) * factor), -32767.0, 32767.0)
            place = lax.broadcasted_iota(jnp.int32, scaled.shape, 0) == rows + HALO - 1
            scaled = jnp.where(place, jnp.broadcast_to(power, scaled.shape), scaled)
            send_ref[d] = scaled.astype(jnp.int32).astype(I16)


def backward(solid_device, solid_patch, flow_p, weights, wall, top, low, high, flow, velocity, heat, devices):
    entries, count = weights.shape
    rows, width = wall.shape
    layers = flow.shape[0]
    tall = devices * rows
    line = pl.BlockSpec((1, CHUNK), lambda i: (0, i))
    fixed = lambda shape: pl.BlockSpec(shape, lambda i: (0,) * len(shape))
    return pl.pallas_call(
        backward_kernel,
        grid=(count // CHUNK,),
        in_specs=[
            line,
            line,
            line,
            pl.BlockSpec((entries, CHUNK), lambda i: (0, i)),
            fixed((rows, width)),
            fixed((2, rows, width)),
            fixed((1, width)),
            fixed((1, width)),
            pl.BlockSpec((1, rows, width), lambda i: (layers - 1, 0, 0)),
            pl.BlockSpec((3, 1, rows, width), lambda i: (0, layers - 1, 0, 0)),
            pl.BlockSpec((1, rows, width), lambda i: (layers - 1, 0, 0)),
        ],
        out_specs=fixed((devices, rows + 8, width)),
        out_shape=jax.ShapeDtypeStruct((devices, rows + 8, width), I16),
        scratch_shapes=[
            pltpu.VMEM((entries, rows * NODES), BF16),
            pltpu.VMEM((entries, rows * NODES), BF16),
            pltpu.VMEM((entries, CHUNK), F32),
            pltpu.VMEM((width, CHUNK), BF16),
            pltpu.VMEM((width, CHUNK), BF16),
            pltpu.VMEM((tall, width), F32),
        ],
        compiler_params=params(),
        cost_estimate=cost(4 * width * (tall + entries) * count, 4 * entries * count),
        name="backward",
    )(solid_device, solid_patch, flow_p, weights, wall, top, low, high, flow, velocity, heat)


def conduct(current, layers, rates, flux):
    rows = current[0].shape[0]
    width = current[0].shape[1]
    out = []
    for l in range(layers):
        centre = current[l]
        low = current[l - 1] if l > 0 else centre
        around = low + pltpu.roll(centre, 1, 0) + pltpu.roll(centre, rows - 1, 0)
        around = around + pltpu.roll(centre, 1, 1) + pltpu.roll(centre, width - 1, 1)
        if l + 1 < len(current):
            around = around + current[l + 1]
        value = centre + CONDUCT_RATE * rates[l] * (around - 6.0 * centre)
        if l == 0 and flux is not None:
            value = value + flux
        out.append(value)
    return out


def rims(pair_ref, cross_ref, l, width):
    low = lax.broadcasted_iota(jnp.int32, (8, width), 0) < HALO
    part = slice(l * 8, l * 8 + 8)
    before, after = sides(pair_ref[part].astype(F32), cross_ref[part].astype(F32))
    return jnp.where(low, after, before), pltpu.roll(jnp.where(low, before, after), HALO, 0)


def liner_kernel(solid_ref, rates_ref, pair_ref, cross_ref, out_ref, first, second, rates):
    layers, rows, width = solid_ref.shape
    for l in range(layers):
        solid_rim, rates_rim = rims(pair_ref, cross_ref, l, width)
        first[l, :rows] = solid_ref[l]
        first[l, rows:] = solid_rim
        rates[l, :rows] = CONDUCT_RATE * rates_ref[l]
        rates[l, rows:] = CONDUCT_RATE * rates_rim
    tall = first.shape[1]

    for substep in range(SUBCYCLES):
        source, target = (first, second) if substep % 2 == 0 else (second, first)
        for l in range(layers):
            centre = source[l]
            around = source[max(l - 1, 0)] + pltpu.roll(centre, 1, 0) + pltpu.roll(centre, tall - 1, 0)
            around = around + pltpu.roll(centre, 1, 1) + pltpu.roll(centre, width - 1, 1)
            if l < layers - 1:
                around = around + source[l + 1]
            value = centre + rates[l] * (around - 6.0 * centre)
            if substep == SUBCYCLES - 1:
                out_ref[l] = value[:rows]
            else:
                target[l] = value


def liner(solid, rates, edge_pair, edge_cross):
    layers, rows, width = solid.shape
    tall = rows + 8
    cells = layers * tall * width
    whole = pl.BlockSpec(solid.shape, lambda i: (0, 0, 0))
    edge = pl.BlockSpec((layers * 8, width), lambda i: (0, 0))
    return pl.pallas_call(
        liner_kernel,
        grid=(1,),
        in_specs=[whole, whole, edge, edge],
        out_specs=whole,
        out_shape=jax.ShapeDtypeStruct(solid.shape, F32),
        scratch_shapes=[pltpu.VMEM((layers, tall, width), F32)] * 3,
        compiler_params=params(),
        cost_estimate=cost(14 * SUBCYCLES * cells, 12 * cells),
        name="liner",
    )(solid, rates, edge_pair, edge_cross)


def liner_top_kernel(arrived_ref, solid_ref, rates_ref, pair_ref, cross_ref, rest_ref, out_ref):
    del rest_ref
    depth, rows, width = solid_ref.shape
    mark = rows + HALO - 1
    flux = jnp.zeros(arrived_ref.shape[1:], F32)
    for d in range(arrived_ref.shape[0]):
        part = arrived_ref[d].astype(jnp.int32).astype(F32)
        flux = flux + part * jnp.exp2(part[mark : mark + 1] - 15.0)
    flux = FLUX_GAIN * flux
    current, rates = [], []
    for l in range(depth):
        solid_rim, rates_rim = rims(pair_ref, cross_ref, l, width)
        current.append(jnp.concatenate([solid_ref[l], solid_rim], axis=0))
        rates.append(jnp.concatenate([rates_ref[l], rates_rim], axis=0))
    for substep in range(SUBCYCLES):
        current = conduct(current, depth - 1 - substep, rates, flux)
    for l in range(SUBCYCLES):
        out_ref[l] = current[l][:rows]


def liner_top(arrived, solid, rates, edge_pair, edge_cross, rest):
    rows, width = solid.shape[1:]
    depth = 2 * SUBCYCLES
    top = pl.BlockSpec((depth, rows, width), lambda i: (0, 0, 0))
    edge = pl.BlockSpec((depth * 8, width), lambda i: (0, 0))
    cells = depth * (rows + 8) * width
    return pl.pallas_call(
        liner_top_kernel,
        grid=(1,),
        in_specs=[
            pl.BlockSpec(arrived.shape, lambda i: (0, 0, 0)),
            top,
            top,
            edge,
            edge,
            pl.BlockSpec(memory_space=pl.ANY),
        ],
        out_specs=pl.BlockSpec((SUBCYCLES, rows, width), lambda i: (0, 0, 0)),
        out_shape=jax.ShapeDtypeStruct(rest.shape, F32),
        input_output_aliases={5: 0},
        compiler_params=params(16 * 1024 * 1024),
        cost_estimate=cost(60 * cells, 8 * cells),
        name="liner_top",
    )(arrived, solid, rates, edge_pair, edge_cross, rest)


def body(
    flow_temp,
    velocity,
    heat_release,
    solid_temp,
    conductivity,
    interp_table,
    flow_patch,
    solid_device,
    solid_patch,
    block_index,
):
    layers, rows, width = flow_temp.shape
    devices = lax.axis_size(AXES)
    near = [(i, i + 1 if i % 2 == 0 else i - 1) for i in range(devices)]
    far = [(i, (i - 1 if i % 2 == 0 else i + 1) % devices) for i in range(devices)]

    steps = jnp.round(solid_temp[0] * STEPS_PER_UNIT).astype(I16)
    outgoing = jnp.broadcast_to(steps[None], (devices, rows, width))
    faces = lax.all_to_all(outgoing, AXES, split_axis=0, concat_axis=0, tiled=True)
    faces = faces.reshape(devices * rows, width)

    to_pair, to_cross = edges(flow_temp, solid_temp, conductivity)
    pair = lax.ppermute(to_pair, AXES, near)
    cross = lax.ppermute(to_cross, AXES, far)

    solid_device = solid_device.reshape(1, -1)
    solid_patch = solid_patch[None]
    flow_p = flow_patch[None]
    weights = weights_of(block_index[None], interp_table.reshape(NODES * NODES, -1))

    wall, top, to_top_pair, to_top_cross = forward(
        solid_device, solid_patch, flow_p, weights, faces, pair, cross, flow_temp, velocity, heat_release
    )
    top_pair = lax.ppermute(to_top_pair, AXES, near)
    top_cross = lax.ppermute(to_top_cross, AXES, far)

    pair, cross, wall = lax.optimization_barrier((pair, cross, wall))
    mid, to_mid_pair, to_mid_cross = predictor(flow_temp, pair, cross, velocity, heat_release)
    mid_pair = lax.ppermute(to_mid_pair, AXES, near)
    mid_cross = lax.ppermute(to_mid_cross, AXES, far)
    top_pair, top_cross, to_mid_pair = lax.optimization_barrier((top_pair, top_cross, to_mid_pair))

    sending = backward(
        solid_device,
        solid_patch,
        flow_p,
        weights,
        wall,
        top,
        top_pair,
        top_cross,
        flow_temp,
        velocity,
        heat_release,
        devices,
    )
    sending, top, pair, mid_pair, mid_cross = lax.optimization_barrier(
        (sending, top, pair, mid_pair, mid_cross)
    )
    arrived = lax.all_to_all(sending, AXES, split_axis=0, concat_axis=0, tiled=True)
    flow_out = corrector(
        mid, top, wall, top_pair, top_cross, mid_pair, mid_cross, flow_temp, velocity, heat_release
    )
    rest = liner(solid_temp, conductivity, pair, cross)
    solid_out = liner_top(arrived, solid_temp, conductivity, pair, cross, rest)
    return (flow_out, solid_out)


def solution(mesh):
    placed = (
        P(None, AXES, None),
        P(None, None, AXES, None),
        P(None, AXES, None),
        P(None, AXES, None),
        P(None, AXES, None),
        P(),
        P(AXES),
        P(AXES, None),
        P(AXES),
        P(AXES),
    )
    return jax.shard_map(
        body,
        mesh=mesh,
        in_specs=placed,
        out_specs=(P(None, AXES, None), P(None, AXES, None)),
        check_vma=False,
    )
```

```python
import functools

import jax
import jax.numpy as jnp
from jax import lax
from jax.experimental import pallas as pl
from jax.experimental.pallas import tpu as pltpu
from jax.sharding import PartitionSpec as P

SUBCYCLES = 4
DIFFUSION = 0.8
TIMESTEP = 0.12
FILM_COEFF = 1.0
CONDUCT_RATE = 0.08
FLUX_GAIN = 0.25

AXES = ("grp", "dom")
NODES = 16
CHUNK = 2048
WEIGHT_CHUNK = 1024
BLOCK = 64
LANES = 128
LAYERS = 16
HALO = 4
F32 = jnp.float32
BF16 = jnp.bfloat16
VMEM_LIMIT = 63 * 1000 * 1000
STEPS_PER_UNIT = 5461.0
I16 = jnp.int16


def params(limit=VMEM_LIMIT):
    return pltpu.CompilerParams(vmem_limit_bytes=limit)


def cost(flops, nbytes):
    return pl.CostEstimate(flops=flops, bytes_accessed=nbytes, transcendentals=0)


def one_hot(index, rows):
    cells = lax.broadcasted_iota(jnp.int16, (rows, index.shape[1]), 0)
    return jnp.where(cells == index.astype(jnp.int16), BF16(1), BF16(0))


def dot(a, b):
    return lax.dot_general(a, b, (((1,), (0,)), ((), ())), preferred_element_type=F32)


def dot_nt(a, b):
    return lax.dot_general(a, b, (((1,), (1,)), ((), ())), preferred_element_type=F32)


def sides(pair, cross):
    even = lax.axis_index(AXES[1]) % 2 == 0
    return jnp.where(even, cross, pair), jnp.where(even, pair, cross)


def lots(to_before, to_after):
    even = lax.axis_index(AXES[1]) % 2 == 0
    return jnp.where(even, to_after, to_before), jnp.where(even, to_before, to_after)


def split(x):
    high = x.astype(BF16)
    return high, (x - high.astype(F32)).astype(BF16)


def stack(x):
    return jnp.concatenate(split(x), axis=0)


def fold(x):
    half = x.shape[0] // 2
    return x[:half] + x[half:]


def weights_kernel(block_ref, table_ref, out_ref, table):
    @pl.when(pl.program_id(0) == 0)
    def _():
        table[...] = stack(table_ref[...])

    picked = one_hot(block_ref[...], table_ref.shape[1])
    out_ref[...] = fold(dot(table[...], picked))


def weights_of(block_index, table):
    entries, blocks = table.shape
    count = block_index.shape[1]
    return pl.pallas_call(
        weights_kernel,
        grid=(count // WEIGHT_CHUNK,),
        in_specs=[
            pl.BlockSpec((1, WEIGHT_CHUNK), lambda i: (0, i)),
            pl.BlockSpec((entries, blocks), lambda i: (0, 0)),
        ],
        out_specs=pl.BlockSpec((entries, WEIGHT_CHUNK), lambda i: (0, i)),
        out_shape=jax.ShapeDtypeStruct((entries, count), F32),
        scratch_shapes=[pltpu.VMEM((2 * entries, blocks), BF16)],
        compiler_params=params(),
        cost_estimate=cost(4 * entries * blocks * count, 4 * entries * (blocks + count)),
        name="weights",
    )(block_index, table)


def spread_rows(rows_x):
    p = lax.broadcasted_iota(jnp.int32, (rows_x, rows_x * NODES), 1)
    x = lax.broadcasted_iota(jnp.int32, (rows_x, rows_x * NODES), 0)
    return jnp.where(p // NODES == x, 1.0, 0.0).astype(BF16)


def patches_to_face(patches, rows_x):
    count = patches.shape[1]
    c = lax.broadcasted_iota(jnp.int32, (NODES, count), 1) % NODES
    parts = [jnp.where(c == k, patches, 0.0) for k in range(NODES)]
    high, low = split(jnp.concatenate(parts, axis=0))
    rows = spread_rows(rows_x)
    return dot_nt(rows, high) + dot_nt(rows, low)


def face_to_patches(face, rows_x):
    high, low = split(face)
    rows = spread_rows(rows_x)
    wide = lax.dot_general(
        high, rows, (((0,), (0,)), ((), ())), preferred_element_type=F32
    ) + lax.dot_general(low, rows, (((0,), (0,)), ((), ())), preferred_element_type=F32)
    c = lax.broadcasted_iota(jnp.int32, (NODES, rows.shape[1]), 1) % NODES
    out = jnp.zeros((NODES, rows.shape[1]), F32)
    for k in range(NODES):
        out = jnp.where(c == k, wide[k * NODES : (k + 1) * NODES], out)
    return out


def solid_place(device_ref, patch_ref, rows_x):
    per_row = NODES
    patch = patch_ref[...]
    return device_ref[...] * rows_x + patch // per_row, patch % per_row


def forward_kernel(
    device_ref,
    patch_ref,
    flow_p_ref,
    weights_ref,
    faces_ref,
    edge_pair_ref,
    edge_cross_ref,
    under_ref,
    flow_ref,
    velocity_ref,
    heat_ref,
    wall_ref,
    top_ref,
    first_ref,
    last_ref,
    faces_turned,
    fetched,
    product,
    total,
):
    step = pl.program_id(0)
    rows_x = wall_ref.shape[0]

    @pl.when(step == 0)
    def _():
        faces_turned[...] = stack(faces_ref[...].astype(F32).T)
        total[...] = jnp.zeros_like(total)

    solid_x, solid_c = solid_place(device_ref, patch_ref, rows_x)
    picked = one_hot(solid_x, faces_ref.shape[0])
    fetched[...] = fold(dot(faces_turned[...], picked))
    for k in range(CHUNK // LANES):
        lanes = slice(k * LANES, (k + 1) * LANES)
        c = jnp.broadcast_to(solid_c[:, lanes], (NODES, LANES))
        values = jnp.zeros((NODES, LANES), F32)
        for j in range(NODES):
            values = jnp.where(c == j, fetched[j * NODES : (j + 1) * NODES, lanes], values)
        values = values * (1.0 / STEPS_PER_UNIT)
        for i in range(NODES):
            rows = slice(i * NODES, (i + 1) * NODES)
            high, low = split(weights_ref[rows, lanes] * values)
            product[rows, lanes] = high
            product[NODES * NODES + i * NODES : NODES * NODES + (i + 1) * NODES, lanes] = low
    placed = one_hot(flow_p_ref[...], total.shape[1])
    total[...] += dot_nt(product[...], placed)

    @pl.when(step == pl.num_programs(0) - 1)
    def _():
        patches = jnp.sum(fold(total[...]).reshape(NODES, NODES, total.shape[1]), axis=1)
        wall = patches_to_face(patches, rows_x)
        wall_ref[...] = wall
        edge = edge_pair_ref.shape[0]
        lows, highs = sides(edge_pair_ref[...].astype(F32), edge_cross_ref[...].astype(F32))
        for l in range(2):
            centre = flow_ref[l]
            zlow = under_ref[1] if l == 0 else flow_ref[0]
            zhigh = flow_ref[1] if l == 0 else wall
            row = slice(edge - 2 + l, edge - 1 + l)
            xlow, xhigh = x_neighbours(centre, lows[row], highs[row])
            vz, vx, vy = (velocity_ref[d, l].astype(F32) for d in range(3))
            top_ref[l] = centre + TIMESTEP * layer_tendency(
                centre, zlow, zhigh, xlow, xhigh, vz, vx, vy, heat_ref[l].astype(F32)
            )
        first_ref[...], last_ref[...] = lots(top_ref[1, :1], top_ref[1, rows_x - 1 :])


def forward(solid_device, solid_patch, flow_p, weights, faces, edge_pair, edge_cross, flow, velocity, heat):
    entries, count = weights.shape
    tall, width = faces.shape
    layers, rows_x = flow.shape[:2]
    last = edge_pair.shape[0] // LAYERS - 1
    edge = pl.BlockSpec((LAYERS, width), lambda i: (last, 0))
    pair = pl.BlockSpec((2, rows_x, width), lambda i: (layers // 2 - 1, 0, 0))
    line = pl.BlockSpec((1, CHUNK), lambda i: (0, i))
    fixed = lambda shape: pl.BlockSpec(shape, lambda i: (0,) * len(shape))
    return pl.pallas_call(
        forward_kernel,
        grid=(count // CHUNK,),
        in_specs=[
            line,
            line,
            line,
            pl.BlockSpec((entries, CHUNK), lambda i: (0, i)),
            fixed((tall, width)),
            edge,
            edge,
            pl.BlockSpec((2, rows_x, width), lambda i: (layers // 2 - 2, 0, 0)),
            pair,
            pl.BlockSpec((3, 2, rows_x, width), lambda i: (0, layers // 2 - 1, 0, 0)),
            pair,
        ],
        out_specs=[fixed((rows_x, width)), fixed((2, rows_x, width)), fixed((1, width)), fixed((1, width))],
        out_shape=[
            jax.ShapeDtypeStruct((rows_x, width), F32),
            jax.ShapeDtypeStruct((2, rows_x, width), F32),
            jax.ShapeDtypeStruct((1, width), F32),
            jax.ShapeDtypeStruct((1, width), F32),
        ],
        scratch_shapes=[
            pltpu.VMEM((2 * width, tall), BF16),
            pltpu.VMEM((width, CHUNK), F32),
            pltpu.VMEM((2 * entries, CHUNK), BF16),
            pltpu.VMEM((2 * entries, rows_x * NODES), F32),
        ],
        compiler_params=params(),
        cost_estimate=cost(4 * width * (tall + entries) * count, 4 * entries * count),
        name="forward",
    )(solid_device, solid_patch, flow_p, weights, faces, edge_pair, edge_cross, flow, flow, velocity, heat)


def edges_kernel(
    flow_low_ref, flow_high_ref, solid_ref, rates_ref, pair_ref, cross_ref
):
    layers = flow_low_ref.shape[0]
    solid_layers, rows, width = solid_ref.shape
    low = lax.broadcasted_iota(jnp.int32, (8, width), 0) < HALO
    for l in range(0, solid_layers, 2):
        ups, downs = [], []
        for m in (l, l + 1):
            ups.append(
                jnp.where(low, pltpu.roll(rates_ref[m, rows - 8 :], HALO, 0), solid_ref[m, rows - 8 :])
            )
            downs.append(jnp.where(low, solid_ref[m, :8], pltpu.roll(rates_ref[m, :8], HALO, 0)))
        pair, cross = lots(jnp.concatenate(downs, axis=0), jnp.concatenate(ups, axis=0))
        pair_ref[l * 8 : l * 8 + 16] = pair.astype(BF16)
        cross_ref[l * 8 : l * 8 + 16] = cross.astype(BF16)
    start = solid_layers * 8
    for l in range(0, layers, LAYERS):
        part = slice(start + l, start + l + LAYERS)
        pair, cross = lots(
            jnp.concatenate([flow_low_ref[m, 0:1] for m in range(l, l + LAYERS)], axis=0),
            jnp.concatenate([flow_high_ref[m, 7:8] for m in range(l, l + LAYERS)], axis=0),
        )
        pair_ref[part] = pair.astype(BF16)
        cross_ref[part] = cross.astype(BF16)


def edges(flow, solid, rates):
    layers, rows, width = flow.shape
    solid_layers = solid.shape[0]
    shape = (solid_layers * 8 + layers, width)
    whole = pl.BlockSpec(solid.shape, lambda i: (0, 0, 0))
    return pl.pallas_call(
        edges_kernel,
        grid=(1,),
        in_specs=[
            pl.BlockSpec((layers, 8, width), lambda i: (0, 0, 0)),
            pl.BlockSpec((layers, 8, width), lambda i: (0, rows // 8 - 1, 0)),
            whole,
            whole,
        ],
        out_specs=[pl.BlockSpec(shape, lambda i: (0, 0))] * 2,
        out_shape=[jax.ShapeDtypeStruct(shape, BF16)] * 2,
        compiler_params=params(),
        cost_estimate=cost(8 * shape[0] * width, 12 * shape[0] * width),
        name="edges",
    )(flow, flow, solid, rates)


def layer_tendency(centre, zlow, zhigh, xlow, xhigh, vz, vx, vy, source):
    width = centre.shape[1]
    total = source
    pairs = (
        (vz, zlow, zhigh),
        (vx, xlow, xhigh),
        (vy, pltpu.roll(centre, 1, 1), pltpu.roll(centre, width - 1, 1)),
    )
    for speed, low, high in pairs:
        a = jnp.maximum(speed, 0.0) + DIFFUSION
        b = a - speed
        total = total + a * (low - centre) + b * (high - centre)
    return total


def x_neighbours(centre, low_row, high_row):
    rows, width = centre.shape
    row = lax.broadcasted_iota(jnp.int32, (rows, width), 0)
    low = jnp.where(row == 0, jnp.broadcast_to(low_row, (rows, width)), pltpu.roll(centre, 1, 0))
    high = jnp.where(
        row == rows - 1, jnp.broadcast_to(high_row, (rows, width)), pltpu.roll(centre, rows - 1, 0)
    )
    return low, high


def predictor_kernel(
    below_ref, flow_ref, above_ref, pair_ref, cross_ref, velocity_ref, heat_ref, out_ref, first_ref, last_ref
):
    step = pl.program_id(0)
    lows, highs = sides(pair_ref[...].astype(F32), cross_ref[...].astype(F32))
    first, last = [], []
    rows = flow_ref.shape[1]
    for l in range(BLOCK):
        centre = flow_ref[l]
        if l == 0:
            zlow = jnp.where(step == 0, 0.0, below_ref[0])
        else:
            zlow = flow_ref[l - 1]
        if l == BLOCK - 1:
            zhigh = jnp.where(step == pl.num_programs(0) - 1, 0.0, above_ref[0])
        else:
            zhigh = flow_ref[l + 1]
        xlow, xhigh = x_neighbours(centre, lows[l : l + 1], highs[l : l + 1])
        vz, vx, vy = (velocity_ref[d, l].astype(F32) for d in range(3))
        value = centre + TIMESTEP * layer_tendency(
            centre, zlow, zhigh, xlow, xhigh, vz, vx, vy, heat_ref[l].astype(F32)
        )
        out_ref[l] = value
        first.append(value[0:1])
        last.append(value[rows - 1 : rows])
    pair, cross = lots(jnp.concatenate(first, axis=0), jnp.concatenate(last, axis=0))
    first_ref[...] = pair.astype(BF16)
    last_ref[...] = cross.astype(BF16)


def layer_specs(shape, halo=True):
    layers, rows, width = shape
    block = pl.BlockSpec((BLOCK, rows, width), lambda i: (i, 0, 0))
    below = pl.BlockSpec((1, rows, width), lambda i: (jnp.maximum(i * BLOCK - 1, 0), 0, 0))
    above = pl.BlockSpec((1, rows, width), lambda i: (jnp.minimum((i + 1) * BLOCK, layers - 1), 0, 0))
    speeds = pl.BlockSpec((3, BLOCK, rows, width), lambda i: (0, i, 0, 0))
    edge = pl.BlockSpec((BLOCK, width), lambda i: (i, 0))
    return block, below, above, speeds, edge


def predictor(flow, low, high, velocity, heat):
    layers, rows, width = flow.shape
    block, below, above, speeds, edge = layer_specs(flow.shape)
    cells = layers * rows * width
    first_edge = (low.shape[0] - layers) // BLOCK
    flow_edge = pl.BlockSpec((BLOCK, width), lambda i: (i + first_edge, 0))
    return pl.pallas_call(
        predictor_kernel,
        grid=(layers // BLOCK,),
        in_specs=[below, block, above, flow_edge, flow_edge, speeds, block],
        out_specs=[block, edge, edge],
        out_shape=[
            jax.ShapeDtypeStruct(flow.shape, F32),
            jax.ShapeDtypeStruct((layers, width), BF16),
            jax.ShapeDtypeStruct((layers, width), BF16),
        ],
        compiler_params=params(),
        cost_estimate=cost(40 * cells, 16 * cells),
        name="predictor",
    )(flow, flow, flow, low, high, velocity, heat)


def corrector_kernel(
    below_ref,
    mid_ref,
    above_ref,
    top_ref,
    wall_ref,
    top_pair_ref,
    top_cross_ref,
    pair_ref,
    cross_ref,
    flow_ref,
    velocity_ref,
    heat_ref,
    out_ref,
):
    step = pl.program_id(0)
    final = step == pl.num_programs(0) - 1
    lows, highs = sides(pair_ref[...].astype(F32), cross_ref[...].astype(F32))
    for l in range(BLOCK):
        centre = mid_ref[l]
        low_row, high_row = lows[l : l + 1], highs[l : l + 1]
        zlow = jnp.where(step == 0, 0.0, below_ref[0]) if l == 0 else mid_ref[l - 1]
        if l == BLOCK - 1:
            centre = jnp.where(final, top_ref[1], centre)
            zhigh = jnp.where(final, wall_ref[...], above_ref[0])
            top_low, top_high = sides(top_pair_ref[...], top_cross_ref[...])
            low_row = jnp.where(final, top_low, low_row)
            high_row = jnp.where(final, top_high, high_row)
        elif l == BLOCK - 2:
            zhigh = jnp.where(final, top_ref[1], mid_ref[l + 1])
        else:
            zhigh = mid_ref[l + 1]
        xlow, xhigh = x_neighbours(centre, low_row, high_row)
        vz, vx, vy = (velocity_ref[d, l].astype(F32) for d in range(3))
        slope = layer_tendency(centre, zlow, zhigh, xlow, xhigh, vz, vx, vy, heat_ref[l].astype(F32))
        out_ref[l] = 0.5 * flow_ref[l] + 0.5 * (centre + TIMESTEP * slope)


def corrector(mid, top, wall, top_low, top_high, low, high, flow, velocity, heat):
    layers, rows, width = flow.shape
    block, below, above, speeds, edge = layer_specs(flow.shape)
    face = pl.BlockSpec((rows, width), lambda i: (0, 0))
    line = pl.BlockSpec((1, width), lambda i: (0, 0))
    cells = layers * rows * width
    return pl.pallas_call(
        corrector_kernel,
        grid=(layers // BLOCK,),
        in_specs=[below, block, above, pl.BlockSpec(top.shape, lambda i: (0, 0, 0)), face, line, line, edge, edge, block, speeds, block],
        out_specs=block,
        out_shape=jax.ShapeDtypeStruct(flow.shape, F32),
        compiler_params=params(),
        cost_estimate=cost(44 * cells, 20 * cells),
        name="corrector",
    )(mid, mid, mid, top, wall, top_low, top_high, low, high, flow, velocity, heat)


def backward_kernel(
    device_ref,
    patch_ref,
    flow_p_ref,
    weights_ref,
    wall_ref,
    top_ref,
    pair_ref,
    cross_ref,
    flow_ref,
    velocity_ref,
    heat_ref,
    send_ref,
    flux_high,
    flux_low,
    fetched,
    returned_high,
    returned_low,
    total,
):
    step = pl.program_id(0)
    rows, width = wall_ref.shape

    @pl.when(step == 0)
    def _():
        total[...] = jnp.zeros_like(total)
        wall = wall_ref[...]
        vz, vx, vy = (velocity_ref[d, 0].astype(F32) for d in range(3))
        top = top_ref[1]
        xlow, xhigh = x_neighbours(top, *sides(pair_ref[...], cross_ref[...]))
        slope = layer_tendency(top, top_ref[0], wall, xlow, xhigh, vz, vx, vy, heat_ref[0].astype(F32))
        out = 0.5 * flow_ref[0] + 0.5 * (top + TIMESTEP * slope)
        patches = face_to_patches(FILM_COEFF * (out - wall), rows)
        wide = jnp.broadcast_to(patches[:, None, :], (NODES, NODES, patches.shape[1]))
        high, low = split(wide.reshape(NODES * NODES, patches.shape[1]))
        flux_high[...] = high
        flux_low[...] = low

    picked = one_hot(flow_p_ref[...], flux_high.shape[1])
    fetched[...] = dot(flux_high[...], picked) + dot(flux_low[...], picked)
    solid_x, solid_c = solid_place(device_ref, patch_ref, rows)
    for k in range(CHUNK // LANES):
        lanes = slice(k * LANES, (k + 1) * LANES)
        value = jnp.zeros((NODES, LANES), F32)
        for i in range(NODES):
            part = slice(i * NODES, (i + 1) * NODES)
            value = value + weights_ref[part, lanes] * fetched[part, lanes]
        c = jnp.broadcast_to(solid_c[:, lanes], (NODES, LANES))
        high, low = split(value)
        high, low = high.astype(F32), low.astype(F32)
        for j in range(NODES):
            part = slice(j * NODES, (j + 1) * NODES)
            returned_high[part, lanes] = jnp.where(c == j, high, 0.0).astype(BF16)
            returned_low[part, lanes] = jnp.where(c == j, low, 0.0).astype(BF16)
    placed = one_hot(solid_x, total.shape[0])
    total[...] += dot_nt(placed, returned_high[...]) + dot_nt(placed, returned_low[...])

    @pl.when(step == pl.num_programs(0) - 1)
    def _():
        devices = send_ref.shape[0]
        tall = total.shape[0]
        peak = jnp.zeros((8, width), F32)
        for r in range(0, tall, 8):
            peak = jnp.maximum(peak, jnp.abs(total[r : r + 8]))
        peak = jnp.maximum(jnp.max(peak, axis=0, keepdims=True), 1e-30)
        power = jnp.floor(jnp.log2(peak)) + 1.0
        factor = jnp.exp2(15.0 - power)
        sub = lax.broadcasted_iota(jnp.int32, (8, width), 0)
        for d in range(devices):
            own = total[d * rows : (d + 1) * rows]
            after = ((d + 1) * rows) % tall
            before = (d * rows - 8) % tall
            rim = jnp.where(sub < HALO, total[after : after + 8], total[before : before + 8])
            scaled = jnp.clip(jnp.round(jnp.concatenate([own, rim], axis=0) * factor), -32767.0, 32767.0)
            place = lax.broadcasted_iota(jnp.int32, scaled.shape, 0) == rows + HALO - 1
            scaled = jnp.where(place, jnp.broadcast_to(power, scaled.shape), scaled)
            send_ref[d] = scaled.astype(jnp.int32).astype(I16)


def backward(solid_device, solid_patch, flow_p, weights, wall, top, low, high, flow, velocity, heat, devices):
    entries, count = weights.shape
    rows, width = wall.shape
    layers = flow.shape[0]
    tall = devices * rows
    line = pl.BlockSpec((1, CHUNK), lambda i: (0, i))
    fixed = lambda shape: pl.BlockSpec(shape, lambda i: (0,) * len(shape))
    return pl.pallas_call(
        backward_kernel,
        grid=(count // CHUNK,),
        in_specs=[
            line,
            line,
            line,
            pl.BlockSpec((entries, CHUNK), lambda i: (0, i)),
            fixed((rows, width)),
            fixed((2, rows, width)),
            fixed((1, width)),
            fixed((1, width)),
            pl.BlockSpec((1, rows, width), lambda i: (layers - 1, 0, 0)),
            pl.BlockSpec((3, 1, rows, width), lambda i: (0, layers - 1, 0, 0)),
            pl.BlockSpec((1, rows, width), lambda i: (layers - 1, 0, 0)),
        ],
        out_specs=fixed((devices, rows + 8, width)),
        out_shape=jax.ShapeDtypeStruct((devices, rows + 8, width), I16),
        scratch_shapes=[
            pltpu.VMEM((entries, rows * NODES), BF16),
            pltpu.VMEM((entries, rows * NODES), BF16),
            pltpu.VMEM((entries, CHUNK), F32),
            pltpu.VMEM((width, CHUNK), BF16),
            pltpu.VMEM((width, CHUNK), BF16),
            pltpu.VMEM((tall, width), F32),
        ],
        compiler_params=params(),
        cost_estimate=cost(4 * width * (tall + entries) * count, 4 * entries * count),
        name="backward",
    )(solid_device, solid_patch, flow_p, weights, wall, top, low, high, flow, velocity, heat)


def conduct(current, layers, rates, flux):
    rows = current[0].shape[0]
    width = current[0].shape[1]
    out = []
    for l in range(layers):
        centre = current[l]
        low = current[l - 1] if l > 0 else centre
        around = low + pltpu.roll(centre, 1, 0) + pltpu.roll(centre, rows - 1, 0)
        around = around + pltpu.roll(centre, 1, 1) + pltpu.roll(centre, width - 1, 1)
        if l + 1 < len(current):
            around = around + current[l + 1]
        value = centre + CONDUCT_RATE * rates[l] * (around - 6.0 * centre)
        if l == 0 and flux is not None:
            value = value + flux
        out.append(value)
    return out


def rims(pair_ref, cross_ref, l, width):
    low = lax.broadcasted_iota(jnp.int32, (8, width), 0) < HALO
    part = slice(l * 8, l * 8 + 8)
    before, after = sides(pair_ref[part].astype(F32), cross_ref[part].astype(F32))
    return jnp.where(low, after, before), pltpu.roll(jnp.where(low, before, after), HALO, 0)


def liner_kernel(solid_ref, rates_ref, pair_ref, cross_ref, out_ref, first, second, rates):
    layers, rows, width = solid_ref.shape
    for l in range(layers):
        solid_rim, rates_rim = rims(pair_ref, cross_ref, l, width)
        first[l, :rows] = solid_ref[l]
        first[l, rows:] = solid_rim
        rates[l, :rows] = CONDUCT_RATE * rates_ref[l]
        rates[l, rows:] = CONDUCT_RATE * rates_rim
    tall = first.shape[1]

    for substep in range(SUBCYCLES):
        source, target = (first, second) if substep % 2 == 0 else (second, first)
        for l in range(layers):
            centre = source[l]
            around = source[max(l - 1, 0)] + pltpu.roll(centre, 1, 0) + pltpu.roll(centre, tall - 1, 0)
            around = around + pltpu.roll(centre, 1, 1) + pltpu.roll(centre, width - 1, 1)
            if l < layers - 1:
                around = around + source[l + 1]
            value = centre + rates[l] * (around - 6.0 * centre)
            if substep == SUBCYCLES - 1:
                out_ref[l] = value[:rows]
            else:
                target[l] = value


def liner(solid, rates, edge_pair, edge_cross):
    layers, rows, width = solid.shape
    tall = rows + 8
    cells = layers * tall * width
    whole = pl.BlockSpec(solid.shape, lambda i: (0, 0, 0))
    edge = pl.BlockSpec((layers * 8, width), lambda i: (0, 0))
    return pl.pallas_call(
        liner_kernel,
        grid=(1,),
        in_specs=[whole, whole, edge, edge],
        out_specs=whole,
        out_shape=jax.ShapeDtypeStruct(solid.shape, F32),
        scratch_shapes=[pltpu.VMEM((layers, tall, width), F32)] * 3,
        compiler_params=params(),
        cost_estimate=cost(14 * SUBCYCLES * cells, 12 * cells),
        name="liner",
    )(solid, rates, edge_pair, edge_cross)


def liner_top_kernel(arrived_ref, solid_ref, rates_ref, pair_ref, cross_ref, rest_ref, out_ref):
    del rest_ref
    depth, rows, width = solid_ref.shape
    mark = rows + HALO - 1
    flux = jnp.zeros(arrived_ref.shape[1:], F32)
    for d in range(arrived_ref.shape[0]):
        part = arrived_ref[d].astype(jnp.int32).astype(F32)
        flux = flux + part * jnp.exp2(part[mark : mark + 1] - 15.0)
    flux = FLUX_GAIN * flux
    current, rates = [], []
    for l in range(depth):
        solid_rim, rates_rim = rims(pair_ref, cross_ref, l, width)
        current.append(jnp.concatenate([solid_ref[l], solid_rim], axis=0))
        rates.append(jnp.concatenate([rates_ref[l], rates_rim], axis=0))
    for substep in range(SUBCYCLES):
        current = conduct(current, depth - 1 - substep, rates, flux)
    for l in range(SUBCYCLES):
        out_ref[l] = current[l][:rows]


def liner_top(arrived, solid, rates, edge_pair, edge_cross, rest):
    rows, width = solid.shape[1:]
    depth = 2 * SUBCYCLES
    top = pl.BlockSpec((depth, rows, width), lambda i: (0, 0, 0))
    edge = pl.BlockSpec((depth * 8, width), lambda i: (0, 0))
    cells = depth * (rows + 8) * width
    return pl.pallas_call(
        liner_top_kernel,
        grid=(1,),
        in_specs=[
            pl.BlockSpec(arrived.shape, lambda i: (0, 0, 0)),
            top,
            top,
            edge,
            edge,
            pl.BlockSpec(memory_space=pl.ANY),
        ],
        out_specs=pl.BlockSpec((SUBCYCLES, rows, width), lambda i: (0, 0, 0)),
        out_shape=jax.ShapeDtypeStruct(rest.shape, F32),
        input_output_aliases={5: 0},
        compiler_params=params(16 * 1024 * 1024),
        cost_estimate=cost(60 * cells, 8 * cells),
        name="liner_top",
    )(arrived, solid, rates, edge_pair, edge_cross, rest)


def body(
    flow_temp,
    velocity,
    heat_release,
    solid_temp,
    conductivity,
    interp_table,
    flow_patch,
    solid_device,
    solid_patch,
    block_index,
):
    layers, rows, width = flow_temp.shape
    devices = lax.axis_size(AXES)
    near = [(i, i + 1 if i % 2 == 0 else i - 1) for i in range(devices)]
    far = [(i, (i - 1 if i % 2 == 0 else i + 1) % devices) for i in range(devices)]

    steps = jnp.round(solid_temp[0] * STEPS_PER_UNIT).astype(I16)
    outgoing = jnp.broadcast_to(steps[None], (devices, rows, width))
    faces = lax.all_to_all(outgoing, AXES, split_axis=0, concat_axis=0, tiled=True)
    faces = faces.reshape(devices * rows, width)

    to_pair, to_cross = edges(flow_temp, solid_temp, conductivity)
    pair = lax.ppermute(to_pair, AXES, near)
    cross = lax.ppermute(to_cross, AXES, far)

    solid_device = solid_device.reshape(1, -1)
    solid_patch = solid_patch[None]
    flow_p = flow_patch[None]
    weights = weights_of(block_index[None], interp_table.reshape(NODES * NODES, -1))

    wall, top, to_top_pair, to_top_cross = forward(
        solid_device, solid_patch, flow_p, weights, faces, pair, cross, flow_temp, velocity, heat_release
    )
    top_pair = lax.ppermute(to_top_pair, AXES, near)
    top_cross = lax.ppermute(to_top_cross, AXES, far)

    pair, cross, wall = lax.optimization_barrier((pair, cross, wall))
    mid, to_mid_pair, to_mid_cross = predictor(flow_temp, pair, cross, velocity, heat_release)
    mid_pair = lax.ppermute(to_mid_pair, AXES, near)
    mid_cross = lax.ppermute(to_mid_cross, AXES, far)
    top_pair, top_cross, to_mid_pair = lax.optimization_barrier((top_pair, top_cross, to_mid_pair))

    sending = backward(
        solid_device,
        solid_patch,
        flow_p,
        weights,
        wall,
        top,
        top_pair,
        top_cross,
        flow_temp,
        velocity,
        heat_release,
        devices,
    )
    sending, top, pair, mid_cross = lax.optimization_barrier((sending, top, pair, mid_cross))
    arrived = lax.all_to_all(sending, AXES, split_axis=0, concat_axis=0, tiled=True)
    flow_out = corrector(
        mid, top, wall, top_pair, top_cross, mid_pair, mid_cross, flow_temp, velocity, heat_release
    )
    rest = liner(solid_temp, conductivity, pair, cross)
    solid_out = liner_top(arrived, solid_temp, conductivity, pair, cross, rest)
    return (flow_out, solid_out)


def solution(mesh):
    placed = (
        P(None, AXES, None),
        P(None, None, AXES, None),
        P(None, AXES, None),
        P(None, AXES, None),
        P(None, AXES, None),
        P(),
        P(AXES),
        P(AXES, None),
        P(AXES),
        P(AXES),
    )
    return jax.shard_map(
        body,
        mesh=mesh,
        in_specs=placed,
        out_specs=(P(None, AXES, None), P(None, AXES, None)),
        check_vma=False,
    )
```
